32 devices in a mesh: rep: 4 (over z), tp: 8 (over y, x, core).
Axes of the slice: x: 2, y: 2, z: 4, core: 2. Of those that a mesh axis runs over, the one named last changes fastest.
Arguments:
- queries: bfloat16 [64, 5, 8192], P('rep', None, 'tp'), may hold values from -120 to 120
- kv_cache: bfloat16 [64, 2, 256, 512], P('rep'), may hold values from -6 to 6
- kv_new: bfloat16 [64, 2, 5, 512], P('rep'), may hold values from -6 to 6
- cache_len: int32 [64], P('rep'), may hold values from 2 to 256, as said below
- out_proj: bfloat16 [8192, 16384], P('tp'), may hold values from -0.09375 to 0.09375
- residual: bfloat16 [64, 5, 16384], P('rep', None, 'tp'), may hold values from -6 to 6
- accepted: int32 [64], P('rep'), may hold values from 0 to 4
- draft_emb: bfloat16 [64, 5, 16384], P('tp'), may hold values from -6 to 6
- draft_gain: bfloat16 [16384], replicated, may hold values from 0.25 to 1.75
- draft_proj: bfloat16 [16384, 16384], P('tp', 'rep'), may hold values from -0.0625 to 0.0625
Outputs:
- verified: bfloat16 [64, 5, 16384], P('rep', None, 'tp')
- draft_features: bfloat16 [64, 16384], P('tp')
The draws below stay inside these ranges and needn't reach their ends.
Inputs may be any that keep to these rules, and one draw needn't show every extreme that they name: `cache_len`: some row has exactly 2 filled slots and some row all 256.
All inputs are finite; a program needn't handle non-finite values.
Results may differ from the reference program's by a relative error of at most 0.0055.
Values may be sent and summed in bfloat16 or wider, within the bound.
A program may use at most 128 MiB of HBM per device.

```python
import jax
import jax.numpy as jnp
from jax import lax

D = 16384
HEADS = 64
KV_HEADS = 4
HEAD_DIM = 128
DRAFT = 5
CACHE = 256
ROWS = 64


def cache_values(key):
    drawn = jax.random.normal(jax.random.fold_in(key, 11), (ROWS, 2, CACHE, KV_HEADS * HEAD_DIM), jnp.float32)
    return jnp.clip(drawn, -6.0, 6.0)


def draw_kv_cache(key, part):
    return cache_values(key).astype(jnp.bfloat16)


def draw_queries(key, part):
    drawn = jnp.clip(jax.random.normal(jax.random.fold_in(key, 12), (ROWS, DRAFT, HEADS * HEAD_DIM), jnp.float32), -6.0, 6.0)
    return drawn.astype(jnp.bfloat16)


def draw_cache_len(key, part):
    lowest = max(2, CACHE // 16)
    lengths = jax.random.randint(jax.random.fold_in(key, 13), (ROWS,), lowest, CACHE + 1)
    return lengths.at[0].set(CACHE).at[1].set(2).astype(jnp.int32)


def draw_accepted(key, part):
    counts = jax.random.randint(jax.random.fold_in(key, 14), (ROWS,), 0, DRAFT)
    return counts.at[0].set(DRAFT - 1).at[1].set(0).astype(jnp.int32)


def raised(array, own_key, source, target, parts, factor):
    owner, partner = [(jnp.arange(array.shape[position]) // (array.shape[position] // parts)).reshape([-1 if axis == position else 1 for axis in range(array.ndim)]) for position in (source, target)]
    chosen = jax.random.permutation(own_key, parts)[partner]
    strong = (owner == chosen) | (owner == (partner + parts // 2) % parts)
    return jnp.where(strong, factor * array, array)


def steps_of(key, shape, shards, smallest, top_value):
    level = 1.0
    for position, blocks in shards:
        steps = jax.random.uniform(jax.random.fold_in(jax.random.fold_in(key, 6), position), (blocks,), jnp.float32, smallest / len(shards), top_value / len(shards))
        level = level * jnp.repeat(jnp.exp(steps), shape[position] // blocks).reshape((-1,) + (1,) * (len(shape) - 1 - position))
    return level


def bell_draw(own_key, extent, deviation, reach, split=(), kind=jnp.bfloat16):
    gain = steps_of(own_key, extent, split, -0.22, 0.18) if split else 1.0
    values = jax.random.normal(own_key, extent, jnp.float32) * deviation * gain
    return jnp.minimum(jnp.maximum(values, -reach), reach).astype(kind)


def noise_with(key, extent, scale, most, shards, heavy, kind=jnp.bfloat16):
    values = scale * jax.random.normal(key, extent, jnp.float32)
    if shards:
        values = values * steps_of(key, extent, shards, -0.22, 0.18)
    return jnp.clip(raised(values, jax.random.fold_in(key, 3), *heavy), -most, most).astype(kind)


def setup_inputs(seed: int = 0) -> dict:
    keys = jax.random.split(jax.random.key(seed), 11)
    queries = draw_queries(jax.random.fold_in(keys[10], 71), 0)
    kv_cache = draw_kv_cache(jax.random.fold_in(keys[10], 71), 0)
    kv_new = bell_draw(keys[2], (ROWS, 2, DRAFT, KV_HEADS * HEAD_DIM), 1.0, 6.0, ((0, 4),))
    cache_len = draw_cache_len(jax.random.fold_in(keys[10], 71), 0)
    out_proj = noise_with(keys[4], (HEADS * HEAD_DIM, D), (HEADS * HEAD_DIM) ** -0.5, 0.09375, ((0, 8),), (0, 1, 8, 2.0))
    residual = bell_draw(keys[5], (ROWS, DRAFT, D), 1.0, 6.0, ((0, 4), (2, 8)))
    accepted = draw_accepted(jax.random.fold_in(keys[10], 71), 0)
    draft_emb = bell_draw(keys[7], (ROWS, DRAFT, D), 1.0, 6.0, ((0, 8),))
    draft_gain = jnp.clip(1.0 + 0.15 * jax.random.normal(keys[8], (D,), jnp.float32), 0.25, 1.75).astype(jnp.bfloat16)
    draft_proj = noise_with(keys[9], (D, D), D ** -0.5, 0.0625, ((0, 8), (1, 4)), (0, 1, 8, 2.0))
    return dict(queries=queries, kv_cache=kv_cache, kv_new=kv_new, cache_len=cache_len, out_proj=out_proj, residual=residual, accepted=accepted, draft_emb=draft_emb, draft_gain=draft_gain, draft_proj=draft_proj)


def attend_row(inputs):
    query_row, cache_row, fresh_row, length_row = inputs
    group = HEADS // KV_HEADS
    scale = HEAD_DIM ** (-0.5)
    query_all = query_row.astype(jnp.float32).reshape(DRAFT, KV_HEADS, group, HEAD_DIM)
    cache_keys = cache_row[0].astype(jnp.float32).reshape(CACHE, KV_HEADS, HEAD_DIM)
    cache_vals = cache_row[1].astype(jnp.float32).reshape(CACHE, KV_HEADS, HEAD_DIM)
    fresh_keys = fresh_row[0].astype(jnp.float32).reshape(DRAFT, KV_HEADS, HEAD_DIM)
    fresh_vals = fresh_row[1].astype(jnp.float32).reshape(DRAFT, KV_HEADS, HEAD_DIM)
    cache_scores = jnp.einsum('jkgd,pkd->jkgp', query_all, cache_keys) * scale
    positions = jnp.arange(CACHE, dtype=jnp.int32)
    cache_scores = jnp.where(positions[None, None, None, :] < length_row, cache_scores, -jnp.inf)
    fresh_scores = jnp.einsum('jkgd,ikd->jkgi', query_all, fresh_keys) * scale
    causal = jnp.arange(DRAFT, dtype=jnp.int32)[None, :] <= jnp.arange(DRAFT, dtype=jnp.int32)[:, None]
    fresh_scores = jnp.where(causal[:, None, None, :], fresh_scores, -jnp.inf)
    highest = jnp.maximum(lax.optimization_barrier(jnp.max(cache_scores, -1)), lax.optimization_barrier(jnp.max(fresh_scores, -1)))[..., None]
    cache_exp = jnp.exp(cache_scores - highest)
    fresh_exp = jnp.exp(fresh_scores - highest)
    total = lax.optimization_barrier(jnp.sum(cache_exp, -1, keepdims=True)) + lax.optimization_barrier(jnp.sum(fresh_exp, -1, keepdims=True))
    cache_weights = (cache_exp / total).astype(jnp.bfloat16)
    fresh_weights = (fresh_exp / total).astype(jnp.bfloat16)
    mixed = jnp.einsum('jkgp,pkd->jkgd', cache_weights.astype(jnp.float32), cache_vals)
    mixed = mixed + jnp.einsum('jkgi,ikd->jkgd', fresh_weights.astype(jnp.float32), fresh_vals)
    return mixed.reshape(DRAFT, HEADS * HEAD_DIM).astype(jnp.bfloat16)

def reference(queries, kv_cache, kv_new, cache_len, out_proj, residual, accepted, draft_emb, draft_gain, draft_proj):
    attn = lax.map(attend_row, (queries, kv_cache, kv_new, cache_len))
    projected = jnp.dot(attn.reshape(ROWS * DRAFT, HEADS * HEAD_DIM), out_proj, preferred_element_type=jnp.float32)
    verified = (residual.astype(jnp.float32) + projected.reshape(ROWS, DRAFT, D)).astype(jnp.bfloat16)
    picked = jnp.arange(DRAFT, dtype=jnp.int32)[None, :] == accepted[:, None]
    feature = lax.optimization_barrier(jnp.sum(jnp.where(picked[:, :, None], verified.astype(jnp.float32), 0.0), axis=1)).astype(jnp.bfloat16)
    state = feature.astype(jnp.float32)
    gain_values = draft_gain.astype(jnp.float32)
    for draft_step in range(DRAFT):
        mixed = state + draft_emb[:, draft_step].astype(jnp.float32)
        inverse = lax.rsqrt(lax.optimization_barrier(jnp.mean(mixed * mixed, axis=1, keepdims=True)) + 1e-05)
        normed = (mixed * inverse * gain_values).astype(jnp.bfloat16)
        update = jnp.dot(normed, draft_proj, preferred_element_type=jnp.float32)
        state = state + jax.nn.silu(update)
    return (verified, state.astype(jnp.bfloat16))
```

```python
import functools

import jax
import jax.numpy as jnp
from jax import lax
from jax.experimental import pallas as pl
from jax.experimental.pallas import tpu as pltpu
from jax.sharding import PartitionSpec as P

KV_HEADS = 4
HEAD_DIM = 128
MESH = pl.DeviceIdType.MESH
F32 = jnp.float32
BF16 = jnp.bfloat16
EXACT = lax.Precision.HIGHEST


def attend(queries, cache_keys, cache_vals, fresh_keys, fresh_vals, cache_len):
    row_count, draft_len, width = queries.shape
    group = width // HEAD_DIM
    scale = HEAD_DIM ** (-0.5)
    query_all = queries.reshape(row_count, draft_len, group, HEAD_DIM)
    cache_scores = (
        jnp.einsum("rjgd,rpd->rjgp", query_all, cache_keys, preferred_element_type=F32) * scale
    )
    positions = jnp.arange(cache_keys.shape[1], dtype=jnp.int32)
    valid = positions[None, :] < cache_len[:, None]
    cache_scores = jnp.where(valid[:, None, None, :], cache_scores, -jnp.inf)
    fresh_scores = (
        jnp.einsum("rjgd,rid->rjgi", query_all, fresh_keys, preferred_element_type=F32) * scale
    )
    causal = jnp.arange(draft_len)[None, :] <= jnp.arange(draft_len)[:, None]
    fresh_scores = jnp.where(causal[None, :, None, :], fresh_scores, -jnp.inf)
    highest = jnp.maximum(jnp.max(cache_scores, -1), jnp.max(fresh_scores, -1))[..., None]
    cache_exp = jnp.exp(cache_scores - highest)
    fresh_exp = jnp.exp(fresh_scores - highest)
    total = jnp.sum(cache_exp, -1, keepdims=True) + jnp.sum(fresh_exp, -1, keepdims=True)
    cache_weights = (cache_exp / total).astype(BF16)
    fresh_weights = (fresh_exp / total).astype(BF16)
    mixed = jnp.einsum("rjgp,rpd->rjgd", cache_weights, cache_vals, preferred_element_type=F32)
    mixed = mixed + jnp.einsum(
        "rjgi,rid->rjgd", fresh_weights, fresh_vals, preferred_element_type=F32
    )
    return mixed.reshape(row_count, draft_len, width).astype(BF16)


def fused(
    T,
    R,
    STEPS,
    attn_ref,
    acc_ref,
    resid_ref,
    racc_ref,
    gain_ref,
    emb_ref,
    oproj_ref,
    dproj_ref,
    ver_ref,
    out_ref,
    w_buf,
    wo_buf,
    ws_buf,
    emb_in,
    emb_f,
    acc_in,
    racc_in,
    part,
    state,
    rs_out,
    rs_in,
    sq_out,
    sq_in,
    z_buf,
    x_buf,
    f_out,
    f_in,
    g_buf,
    v_out,
    v_in,
    w_sem,
    wo_sem,
    ws_sem,
    e_send,
    e_recv,
    a_send,
    a_recv,
    ra_send,
    ra_recv,
    rs_send,
    rs_recv,
    sq_send,
    sq_recv,
    z_send,
    z_recv,
    x_send,
    x_recv,
    f_send,
    f_recv,
    g_send,
    g_recv,
    v_send,
    v_recv,
):
    t = lax.axis_index("tp")
    r = lax.axis_index("rep")
    ratio = T // R
    rows, cw = state.shape
    width = gain_ref.shape[1]
    kb = width // T
    nb = width // R
    own_rows = rows // T
    rr = acc_ref.shape[0]

    def plane(k):
        return lax.rem(t + k, T)

    def tower(j):
        return lax.rem(r + j, R)

    def tower_back(j):
        return lax.rem(r - j + R, R)

    def remote(src, dst, send, recv, axis, index):
        return pltpu.make_async_remote_copy(
            src_ref=src,
            dst_ref=dst,
            send_sem=send,
            recv_sem=recv,
            device_id={axis: index},
            device_id_type=MESH,
        )

    def cols(start, size):
        return pl.ds(pl.multiple_of(start, 128), size)

    wo_copy = pltpu.make_async_copy(oproj_ref.at[:, cols(r * nb, nb)], wo_buf, wo_sem)
    wo_copy.start()

    def ws_copy(kk, slot):
        return pltpu.make_async_copy(
            oproj_ref.at[:, cols(plane(kk + 1) * kb, kb)], ws_buf.at[slot], ws_sem.at[slot]
        )

    barrier = pltpu.get_barrier_semaphore()
    for k in range(1, T):
        pl.semaphore_signal(barrier, inc=1, device_id={"tp": plane(k)}, device_id_type=MESH)
    for j in range(1, R):
        pl.semaphore_signal(barrier, inc=1, device_id={"rep": tower(j)}, device_id_type=MESH)
    pl.semaphore_wait(barrier, T - 1 + R - 1)

    def a_copy(j):
        return remote(acc_ref, acc_in.at[r], a_send.at[j], a_recv.at[j], "rep", tower(j))

    for j in range(1, R):
        a_copy(j).start()
    acc_in[r] = acc_ref[...]

    home = t // ratio
    ra_offset = lax.rem(home - r + R, R)

    def ra_copy():
        return remote(racc_ref, racc_in.at[r], ra_send, ra_recv.at[ra_offset], "rep", home)

    @pl.when(home != r)
    def _():
        ra_copy().start()

    @pl.when(home == r)
    def _():
        racc_in[r] = racc_ref[...]

    w_copy = pltpu.make_async_copy(dproj_ref, w_buf, w_sem)
    w_copy.start()

    def e_copy(k):
        return remote(
            emb_ref.at[:, cols((r * T + plane(k)) * cw, cw)],
            emb_in.at[k],
            e_send.at[k],
            e_recv.at[k],
            "tp",
            plane(k),
        )

    e_own = pltpu.make_async_copy(
        emb_ref.at[:, cols((r * T + t) * cw, cw)], emb_in.at[0], e_send.at[0]
    )
    e_own.start()

    for k in range(1, T):
        e_copy(k).start()
    ws_copy(0, 0).start()
    ws_copy(1, 1).start()

    for j in range(1, R):
        a_copy(j).wait_recv()

    @pl.when(home == r)
    def _():
        for j in range(1, R):
            remote(
                racc_ref, racc_in.at[tower_back(j)], ra_send, ra_recv.at[j], "rep", tower(j)
            ).wait_recv()

    wo_copy.wait()

    def rs_copy(i, k):
        return remote(
            rs_out.at[k], rs_in.at[i, k], rs_send.at[k], rs_recv.at[i, k], "tp", plane(k)
        )

    def finish(i):
        for k in range(1, T):
            rs_copy(i, k).wait_recv()
        total = rs_in[i, 0].astype(F32)
        for k in range(1, T):
            total = total + rs_in[i, k].astype(F32)
        for k in range(1, T):
            rs_copy(i, k).wait_send()
        return total

    first = acc_in[...].reshape(rows, acc_ref.shape[1])

    def project(kk, _):
        k = lax.rem(kk + 1, T)
        c = plane(k)
        part[...] = jnp.dot(first, wo_buf[:, cols(c * cw, cw)], preferred_element_type=F32)

        @pl.when(r * ratio + c // R == t)
        def _():
            part[...] += (
                racc_in[:, :, cols(lax.rem(c, R) * cw, cw)].reshape(rows, cw).astype(F32)
            )

        @pl.when(kk < T - 1)
        def _():
            rs_out[k] = part[...].astype(BF16)
            rs_copy(0, k).start()

        @pl.when(kk == T - 1)
        def _():
            rs_in[0, 0] = part[...].astype(BF16)

        return 0

    lax.fori_loop(0, T, project, 0)

    e_own.wait()
    for k in range(1, T):
        e_copy(k).wait_recv()

    def place(k, _):
        source = lax.rem(t - k + T, T)
        block = emb_in[k].astype(F32)
        for s in range(STEPS):
            emb_f[s, pl.ds(pl.multiple_of(source * own_rows, own_rows), own_rows), :] = block[
                s * own_rows : (s + 1) * own_rows
            ]
        return 0

    lax.fori_loop(0, T, place, 0)
    state[...] = finish(0).astype(BF16).astype(F32)
    w_copy.wait()

    gain_own = gain_ref[:, cols((r * T + t) * cw, cw)]
    gain_back = 1.0 / gain_ref[:, cols(t * kb, kb)]

    vb = min(kb, 512)

    def v_copy(kk):
        return remote(
            v_out.at[kk], v_in.at[kk], v_send.at[kk], v_recv.at[kk], "tp", plane(kk + 1)
        )

    def v_chunk(kk):
        slot = lax.rem(kk, 2)
        ws_copy(kk, slot).wait()

        def block(b, _):
            here = cols(b * vb, vb)
            v_out[kk, :, here] = jnp.dot(
                attn_ref[...], ws_buf[slot, :, here], preferred_element_type=F32
            ).astype(BF16)
            return 0

        lax.fori_loop(0, kb // vb, block, 0)

        @pl.when(kk < T - 1)
        def _():
            v_copy(kk).start()

        @pl.when(kk < T - 2)
        def _():
            ws_copy(kk + 2, slot).start()

    gaps = 2 * (STEPS - 1)
    per_gap = -(-T // gaps)

    def v_gap(g):
        for n in range(per_gap):
            kk = g * per_gap + n

            @pl.when(kk < T)
            def _():
                v_chunk(kk)

    def x_copy(s, j):
        q = tower_back(j)
        target = q * ratio + t // R
        m = lax.rem(t, R)
        return target, remote(
            z_buf.at[s, q], x_buf.at[s, m], x_send.at[j], x_recv.at[s, m], "tp", target
        )

    def z_copy(s, j):
        return remote(z_buf.at[s, r], z_buf.at[s, r], z_send.at[j], z_recv.at[s, j], "rep", tower(j))

    def z_arrival(s, j):
        q = tower_back(j)
        return remote(z_buf.at[s, q], z_buf.at[s, q], z_send.at[j], z_recv.at[s, j], "rep", tower(j))

    def sq_copy(s, k):
        return remote(
            sq_out, sq_in.at[s, k], sq_send.at[k], sq_recv.at[s, k], "tp", plane(k)
        )

    def step(s, _):
        mixed = state[...] + emb_f[s]
        z_buf[s, r] = (mixed * gain_own).astype(BF16)
        for j in range(1, R):
            z_copy(s, j).start()
        for j in range(R):
            if j == 1:
                v_gap(2 * s)
            if j > 0:
                z_arrival(s, j).wait_recv()
            target, copy = x_copy(s, j)

            @pl.when(target != t)
            def _():
                copy.start()

            @pl.when(target == t)
            def _():
                x_buf[s, lax.rem(t, R)] = z_buf[s, tower_back(j)]

        for m in range(R):
            source = lax.rem(t, ratio) * R + m

            @pl.when(source != t)
            def _():
                remote(
                    z_buf.at[s, 0], x_buf.at[s, m], x_send.at[0], x_recv.at[s, m], "tp", source
                ).wait_recv()

        x = jnp.concatenate([x_buf[s, m] for m in range(R)], axis=1)
        plain = x.astype(F32) * gain_back
        plain = plain * plain
        lanes = plain[:, :128]
        for b in range(1, kb // 128):
            lanes = lanes + plain[:, b * 128 : (b + 1) * 128]
        sq_out[:, :rows] = lax.dot_general(
            jnp.ones((8, 128), F32),
            lanes,
            (((1,), (1,)), ((), ())),
            precision=EXACT,
            preferred_element_type=F32,
        )
        for k in range(1, T):
            sq_copy(s, k).start()
        sq_in[s, 0] = sq_out[...]

        def multiply(kk, _):
            k = lax.rem(kk + 1, T)
            product = jnp.dot(
                x, w_buf[:, cols(plane(k) * cw, cw)], preferred_element_type=F32
            ).astype(BF16)

            @pl.when(kk < T - 1)
            def _():
                rs_out[k] = product
                rs_copy(s + 1, k).start()

            @pl.when(kk == T - 1)
            def _():
                rs_in[s + 1, 0] = product

            return 0

        lax.fori_loop(0, T, multiply, 0)
        v_gap(2 * s + 1)
        for k in range(1, T):
            sq_copy(s, k).wait_recv()
        squares = sq_in[s, 0]
        for k in range(1, T):
            squares = squares + sq_in[s, k]
        column = lax.dot_general(
            squares,
            jnp.full((8, 128), 0.125, F32),
            (((0,), (0,)), ((), ())),
            precision=EXACT,
            preferred_element_type=F32,
        )[:rows, :1]
        inverse = lax.rsqrt(column / width + 1e-05)
        update = finish(s + 1) * inverse
        state[...] += update / (1.0 + jnp.exp(-update))
        for k in range(1, T):
            sq_copy(s, k).wait_send()
        for j in range(1, R):
            z_copy(s, j).wait_send()
        for j in range(R):
            target, copy = x_copy(s, j)

            @pl.when(target != t)
            def _():
                copy.wait_send()

        return 0

    sq_out[...] = jnp.zeros_like(sq_out)
    lax.fori_loop(0, STEPS, step, 0)

    def f_copy(k):
        return remote(f_out.at[k], f_in.at[t], f_send.at[k], f_recv.at[k], "tp", plane(k))

    blank = jnp.zeros((16 - own_rows, cw), F32)
    for k in range(T):
        here = pl.ds(pl.multiple_of(plane(k) * own_rows, own_rows), own_rows)
        f_out[k] = jnp.concatenate([state[here, :], blank], axis=0).astype(BF16)
        if k > 0:
            f_copy(k).start()
    f_in[t] = f_out[0]

    def v_wait(kk, _):
        remote(
            v_out.at[kk], v_in.at[kk], v_send.at[kk], v_recv.at[kk], "tp", plane(kk + 1)
        ).wait()
        return 0

    for k in range(1, T):
        remote(
            f_out.at[k],
            f_in.at[lax.rem(t - k + T, T)],
            f_send.at[k],
            f_recv.at[k],
            "tp",
            plane(k),
        ).wait()
    half = T // 2
    for k in range(half):
        top = f_in[k].astype(F32)[:own_rows]
        low = f_in[k + half].astype(F32)[:own_rows]
        g_buf[r, :, k * cw : (k + 1) * cw] = jnp.concatenate([top, low], axis=0).astype(BF16)

    def g_copy(j):
        return remote(g_buf.at[r], g_buf.at[r], g_send.at[j], g_recv.at[j], "rep", tower(j))

    for j in range(1, R):
        g_copy(j).start()

    lax.fori_loop(0, T - 1, v_wait, 0)

    def v_sum(b, _):
        here = cols(b * vb, vb)
        total = v_out[T - 1, :, here].astype(F32)
        for kk in range(T - 1):
            total = total + v_in[kk, :, here].astype(F32)
        ver_ref[:, here] = (resid_ref[:, here].astype(F32) + total).astype(BF16)
        return 0

    lax.fori_loop(0, kb // vb, v_sum, 0)

    for j in range(1, R):
        q = tower_back(j)
        remote(g_buf.at[q], g_buf.at[q], g_send.at[j], g_recv.at[j], "rep", tower(j)).wait()
    for q in range(R):
        block = g_buf[q].astype(F32)
        out_ref[:, q * nb : q * nb + nb // 2] = block[:own_rows].astype(BF16)
        out_ref[:, q * nb + nb // 2 : (q + 1) * nb] = block[own_rows:].astype(BF16)

    for j in range(1, R):
        a_copy(j).wait_send()

    @pl.when(home != r)
    def _():
        ra_copy().wait_send()

    for k in range(1, T):
        e_copy(k).wait_send()


def local(
    T,
    R,
    queries,
    kv_cache,
    kv_new,
    cache_len,
    out_proj,
    residual,
    accepted,
    draft_emb,
    draft_gain,
    draft_proj,
):
    row_count, draft_len, kdim = queries.shape
    width = draft_gain.shape[0]
    rows = row_count * R
    own_rows, steps = draft_emb.shape[:2]
    cw = width // (T * R)
    kb = width // T
    nb = width // R
    group = kdim * T // HEAD_DIM // KV_HEADS
    kv_start = lax.axis_index("tp") * (kdim // HEAD_DIM) // group * HEAD_DIM
    own_cache = lax.dynamic_slice_in_dim(kv_cache, kv_start, HEAD_DIM, 3)
    own_fresh = lax.dynamic_slice_in_dim(kv_new, kv_start, HEAD_DIM, 3)
    attn = attend(
        queries, own_cache[:, 0], own_cache[:, 1], own_fresh[:, 0], own_fresh[:, 1], cache_len
    )
    picked = (jnp.arange(draft_len, dtype=jnp.int32)[None, :] == accepted[:, None])[:, :, None]

    def pick(array):
        return jnp.sum(jnp.where(picked, array.astype(F32), 0.0), axis=1).astype(BF16)

    emb = draft_emb.transpose(1, 0, 2).reshape(steps * own_rows, width)
    emb_rows = -(-steps * own_rows // 16) * 16
    emb = jnp.pad(emb, ((0, emb_rows - steps * own_rows), (0, 0)))
    token_rows = row_count * draft_len
    dma = pltpu.SemaphoreType.DMA
    vmem = pl.BlockSpec(memory_space=pltpu.VMEM)
    hbm = pl.BlockSpec(memory_space=pl.ANY)
    verified, features = pl.pallas_call(
        functools.partial(fused, T, R, steps),
        out_shape=(
            jax.ShapeDtypeStruct((token_rows, kb), BF16),
            jax.ShapeDtypeStruct((own_rows, width), BF16),
        ),
        in_specs=[vmem] * 5 + [hbm] * 3,
        out_specs=(vmem, vmem),
        scratch_shapes=[
            pltpu.VMEM((kb, nb), BF16),
            pltpu.VMEM((kdim, nb), BF16),
            pltpu.VMEM((2, kdim, kb), BF16),
            pltpu.VMEM((T, emb_rows, cw), BF16),
            pltpu.VMEM((steps, rows, cw), F32),
            pltpu.VMEM((R, row_count, kdim), BF16),
            pltpu.VMEM((R, row_count, kb), BF16),
            pltpu.VMEM((rows, cw), F32),
            pltpu.VMEM((rows, cw), F32),
            pltpu.VMEM((T, rows, cw), BF16),
            pltpu.VMEM((steps + 1, T, rows, cw), BF16),
            pltpu.VMEM((8, 128), F32),
            pltpu.VMEM((steps, T, 8, 128), F32),
            pltpu.VMEM((steps, R, rows, cw), BF16),
            pltpu.VMEM((steps, R, rows, cw), BF16),
            pltpu.VMEM((T, 16, cw), BF16),
            pltpu.VMEM((T, 16, cw), BF16),
            pltpu.VMEM((R, 16, nb // 2), BF16),
            pltpu.VMEM((T, token_rows, kb), BF16),
            pltpu.VMEM((T, token_rows, kb), BF16),
            dma,
            dma,
            dma((2,)),
            dma((T,)),
            dma((T,)),
            dma((R,)),
            dma((R,)),
            dma,
            dma((R,)),
            dma((T,)),
            dma((steps + 1, T)),
            dma((T,)),
            dma((steps, T)),
            dma((R,)),
            dma((steps, R)),
            dma((R,)),
            dma((steps, R)),
            dma((T,)),
            dma((T,)),
            dma((R,)),
            dma((R,)),
            dma((T,)),
            dma((T,)),
        ],
        compiler_params=pltpu.CompilerParams(
            collective_id=0, has_side_effects=True, vmem_limit_bytes=56 * 2**20
        ),
        name="verify_and_draft",
    )(
        attn.reshape(token_rows, kdim),
        pick(attn),
        residual.reshape(token_rows, kb),
        pick(residual),
        draft_gain.astype(F32).reshape(1, width),
        emb,
        out_proj,
        draft_proj,
    )
    return verified.reshape(row_count, draft_len, kb), features


def solution(mesh):
    in_specs = (
        P("rep", None, "tp"),
        P("rep", None, None, None),
        P("rep", None, None, None),
        P("rep"),
        P("tp", None),
        P("rep", None, "tp"),
        P("rep"),
        P("tp", None, None),
        P(),
        P("tp", "rep"),
    )
    out_specs = (P("rep", None, "tp"), P("tp", None))
    body = functools.partial(local, mesh.shape["tp"], mesh.shape["rep"])
    return jax.shard_map(body, mesh=mesh, in_specs=in_specs, out_specs=out_specs, check_vma=False)
```

```python
import functools

import jax
import jax.numpy as jnp
from jax import lax
from jax.experimental import pallas as pl
from jax.experimental.pallas import tpu as pltpu
from jax.sharding import PartitionSpec as P

KV_HEADS = 4
HEAD_DIM = 128
MESH = pl.DeviceIdType.MESH
F32 = jnp.float32
BF16 = jnp.bfloat16
EXACT = lax.Precision.HIGHEST


def fused(
    T,
    R,
    STEPS,
    len_ref,
    pick_ref,
    q_ref,
    fresh_ref,
    resid_ref,
    gain_ref,
    kv_ref,
    emb_ref,
    oproj_ref,
    dproj_ref,
    ver_ref,
    out_ref,
    kv_buf,
    padded,
    attn_ref,
    acc_ref,
    racc_f,
    racc_ref,
    w_buf,
    wo_buf,
    ws_buf,
    emb_in,
    emb_f,
    acc_in,
    racc_in,
    part,
    state,
    rs_out,
    rs_in,
    sq_out,
    sq_in,
    z_buf,
    x_buf,
    f_out,
    f_in,
    g_buf,
    p_out,
    p_in,
    v_out,
    v_in,
    kv_sem,
    w_sem,
    wo_sem,
    ws_sem,
    e_send,
    e_recv,
    a_send,
    a_recv,
    ra_send,
    ra_recv,
    rs_send,
    rs_recv,
    sq_send,
    sq_recv,
    z_send,
    z_recv,
    x_send,
    x_recv,
    f_send,
    f_recv,
    g_send,
    g_recv,
    p_send,
    p_recv,
    v_send,
    v_recv,
):
    t = lax.axis_index("tp")
    r = lax.axis_index("rep")
    ratio = T // R
    rows, cw = state.shape
    width = gain_ref.shape[1]
    kb = width // T
    nb = width // R
    own_rows = rows // T
    rr, draft_len, kdim = q_ref.shape
    heads = kdim // HEAD_DIM
    chips = T // 2
    core = lax.rem(t, 2)
    chip = t // 2
    halves, hw = x_buf.shape[1] // R, x_buf.shape[3]

    def plane(k):
        return lax.rem(t + k, T)

    def flip(index, k, limit):
        out, bit = 0, 1
        while bit < limit:
            out = out + bit * lax.rem(index // bit + k // bit, 2)
            bit *= 2
        return out

    def tower(j):
        return lax.rem(r + j, R)

    def tower_back(j):
        return lax.rem(r - j + R, R)

    def remote(src, dst, send, recv, axis, index):
        return pltpu.make_async_remote_copy(
            src_ref=src,
            dst_ref=dst,
            send_sem=send,
            recv_sem=recv,
            device_id={axis: index},
            device_id_type=MESH,
        )

    def cols(start, size):
        return pl.ds(pl.multiple_of(start, 128), size)

    kv_group = t * heads // (heads * T // KV_HEADS)
    kv_copy = pltpu.make_async_copy(
        kv_ref.at[:, :, :, cols(kv_group * HEAD_DIM, HEAD_DIM)], kv_buf, kv_sem
    )
    kv_copy.start()
    wo_copy = pltpu.make_async_copy(oproj_ref.at[:, cols(r * nb, nb)], wo_buf, wo_sem)
    wo_copy.start()

    def turn(n, own):
        k = chips - 1 - n
        swapped = (k // 4) * 4 + lax.rem(k, 2) * 2 + lax.rem(k // 2, 2)
        return k + (core if own else 1 - core) * (swapped - k)

    def served(n, own):
        return flip(chip, turn(n, own), chips) * 2 + (core if own else 1 - core)

    def ws_copy(n, own):
        return pltpu.make_async_copy(
            oproj_ref.at[:, cols(served(n, own) * kb, kb)], ws_buf.at[own], ws_sem.at[own]
        )

    def pick_row(n, _):
        block = resid_ref[n].astype(F32)
        chosen = lax.broadcasted_iota(jnp.int32, block.shape, 0) == pick_ref[n]
        racc_f[pl.ds(n, 1), :] = jnp.sum(jnp.where(chosen, block, 0.0), axis=0, keepdims=True)
        return 0

    lax.fori_loop(0, rr, pick_row, 0)
    racc_ref[...] = racc_f[...].astype(BF16)

    barrier = pltpu.get_barrier_semaphore()
    for k in range(1, T):
        pl.semaphore_signal(barrier, inc=1, device_id={"tp": plane(k)}, device_id_type=MESH)
    for j in range(1, R):
        pl.semaphore_signal(barrier, inc=1, device_id={"rep": tower(j)}, device_id_type=MESH)
    pl.semaphore_wait(barrier, T - 1 + R - 1)

    home = t // ratio
    ra_offset = lax.rem(home - r + R, R)

    def ra_copy():
        return remote(racc_ref, racc_in.at[r], ra_send, ra_recv.at[ra_offset], "rep", home)

    @pl.when(home != r)
    def _():
        ra_copy().start()

    @pl.when(home == r)
    def _():
        racc_in[r] = racc_ref[...]

    w_copy = pltpu.make_async_copy(dproj_ref, w_buf, w_sem)
    w_copy.start()

    def e_copy(k):
        return remote(
            emb_ref.at[:, cols((r * T + plane(k)) * cw, cw)],
            emb_in.at[k],
            e_send.at[k],
            e_recv.at[k],
            "tp",
            plane(k),
        )

    e_own = pltpu.make_async_copy(
        emb_ref.at[:, cols((r * T + t) * cw, cw)], emb_in.at[0], e_send.at[0]
    )
    e_own.start()

    for k in range(1, T):
        e_copy(k).start()
    ws_copy(0, 0).start()
    ws_copy(0, 1).start()

    kv_copy.wait()
    tall = 8 * heads
    scale = HEAD_DIM ** (-0.5)
    token = lax.rem(lax.broadcasted_iota(jnp.int32, (tall, 128), 0), 8)
    fresh_ok = lax.broadcasted_iota(jnp.int32, (tall, 128), 1) <= token
    slots = kv_buf.shape[2]
    slot_at = lax.broadcasted_iota(jnp.int32, (tall, slots), 1)
    across = (((1,), (1,)), ((), ()))
    fresh_cols = cols(kv_group * HEAD_DIM, HEAD_DIM)
    empty = jnp.zeros((8 - draft_len, kdim), F32)
    unused = jnp.zeros((128 - draft_len, HEAD_DIM), F32)

    def attend_row(n, _):
        query = jnp.concatenate([q_ref[n].astype(F32), empty], axis=0)
        query = jnp.concatenate(
            [query[:, h * HEAD_DIM : (h + 1) * HEAD_DIM] for h in range(heads)], axis=0
        ).astype(BF16)
        fresh_keys = jnp.concatenate(
            [fresh_ref[n, 0, :, fresh_cols].astype(F32), unused], axis=0
        ).astype(BF16)
        fresh_vals = jnp.concatenate(
            [fresh_ref[n, 1, :, fresh_cols].astype(F32), unused], axis=0
        ).astype(BF16)
        cache_scores = (
            lax.dot_general(query, kv_buf[n, 0], across, preferred_element_type=F32) * scale
        )
        fresh_scores = (
            lax.dot_general(query, fresh_keys, across, preferred_element_type=F32) * scale
        )
        cache_scores = jnp.where(slot_at < len_ref[n], cache_scores, -jnp.inf)
        fresh_scores = jnp.where(fresh_ok, fresh_scores, -jnp.inf)
        highest = jnp.maximum(
            jnp.max(cache_scores, axis=1, keepdims=True),
            jnp.max(fresh_scores, axis=1, keepdims=True),
        )
        cache_exp = jnp.exp(cache_scores - highest)
        fresh_exp = jnp.exp(fresh_scores - highest)
        total = jnp.sum(cache_exp, axis=1, keepdims=True) + jnp.sum(
            fresh_exp, axis=1, keepdims=True
        )
        mixed = jnp.dot(
            (cache_exp / total).astype(BF16), kv_buf[n, 1], preferred_element_type=F32
        ) + jnp.dot((fresh_exp / total).astype(BF16), fresh_vals, preferred_element_type=F32)
        padded[pl.ds(pl.multiple_of(n * 8, 8), 8), :] = jnp.concatenate(
            [mixed[h * 8 : (h + 1) * 8] for h in range(heads)], axis=1
        )
        return 0

    lax.fori_loop(0, rr, attend_row, 0, unroll=4)

    attended = padded[...].astype(BF16)
    row_at = lax.broadcasted_iota(jnp.int32, (rr, 8 * rr), 0)
    target = row_at * 8
    for n in range(rr):
        target = jnp.where(row_at == n, 8 * n + pick_ref[n], target)
    chosen = lax.broadcasted_iota(jnp.int32, (rr, 8 * rr), 1) == target
    acc_ref[...] = jnp.dot(
        jnp.where(chosen, 1.0, 0.0).astype(BF16), attended, preferred_element_type=F32
    ).astype(BF16)

    def a_copy(j):
        return remote(acc_ref, acc_in.at[r], a_send.at[j], a_recv.at[j], "rep", tower(j))

    for j in range(1, R):
        a_copy(j).start()
    acc_in[r] = acc_ref[...]

    token_at = lax.broadcasted_iota(jnp.int32, (rr * draft_len, 8 * rr), 0)
    place_at = lax.broadcasted_iota(jnp.int32, (rr * draft_len, 8 * rr), 1)
    kept = (token_at == place_at - (8 - draft_len) * (place_at // 8)) & (
        lax.rem(place_at, 8) < draft_len
    )
    attn_ref[...] = jnp.dot(
        jnp.where(kept, 1.0, 0.0).astype(BF16), attended, preferred_element_type=F32
    ).astype(BF16)


    for j in range(1, R):
        a_copy(j).wait_recv()

    @pl.when(home == r)
    def _():
        for j in range(1, R):
            remote(
                racc_ref, racc_in.at[tower_back(j)], ra_send, ra_recv.at[j], "rep", tower(j)
            ).wait_recv()

    wo_copy.wait()

    def rs_copy(i, k):
        return remote(
            rs_out.at[k], rs_in.at[i, k], rs_send.at[k], rs_recv.at[i, k], "tp", flip(t, k, T)
        )

    def finish(i):
        for k in range(1, T):
            rs_copy(i, k).wait_recv()
        total = rs_in[i, 0].astype(F32)
        for k in range(1, T):
            total = total + rs_in[i, k].astype(F32)
        for k in range(1, T):
            rs_copy(i, k).wait_send()
        return total

    first = acc_in[...].reshape(rows, acc_ref.shape[1])

    def project(kk, _):
        k = T - 1 - kk
        c = flip(t, k, T)
        part[...] = jnp.dot(first, wo_buf[:, cols(c * cw, cw)], preferred_element_type=F32)

        @pl.when(r * ratio + c // R == t)
        def _():
            part[...] += (
                racc_in[:, :, cols(lax.rem(c, R) * cw, cw)].reshape(rows, cw).astype(F32)
            )

        @pl.when(kk < T - 1)
        def _():
            rs_out[k] = part[...].astype(BF16)
            rs_copy(0, k).start()

        @pl.when(kk == T - 1)
        def _():
            rs_in[0, 0] = part[...].astype(BF16)

        return 0

    lax.fori_loop(0, T, project, 0)

    e_own.wait()
    for k in range(1, T):
        e_copy(k).wait_recv()

    def place(k, _):
        source = lax.rem(t - k + T, T)
        block = emb_in[k].astype(F32)
        for s in range(STEPS):
            emb_f[s, pl.ds(pl.multiple_of(source * own_rows, own_rows), own_rows), :] = block[
                s * own_rows : (s + 1) * own_rows
            ]
        return 0

    lax.fori_loop(0, T, place, 0)
    state[...] = finish(0).astype(BF16).astype(F32)
    w_copy.wait()

    gain_own = gain_ref[:, cols((r * T + t) * cw, cw)]
    gain_back = 1.0 / gain_ref[:, cols(t * kb, kb)]

    vb = min(kb, 512)

    def p_copy(n):
        return remote(
            p_out.at[n], p_in.at[n], p_send.at[n], p_recv.at[n], "tp", chip * 2 + 1 - core
        )

    def v_copy(n):
        return remote(
            v_out.at[n], v_in.at[n], v_send.at[n], v_recv.at[n], "tp", served(n, True)
        )

    def v_other(n):
        ws_copy(n, 0).wait()

        def block(b, _):
            here = cols(b * vb, vb)
            p_out[n, :, here] = jnp.dot(
                attn_ref[...], ws_buf[0, :, here], preferred_element_type=F32
            ).astype(BF16)
            return 0

        lax.fori_loop(0, kb // vb, block, 0)
        p_copy(n).start()

        @pl.when(n < chips - 1)
        def _():
            ws_copy(n + 1, 0).start()

    def v_own(n):
        ws_copy(n, 1).wait()
        p_copy(n).wait_recv()

        def block(b, _):
            here = cols(b * vb, vb)
            product = jnp.dot(attn_ref[...], ws_buf[1, :, here], preferred_element_type=F32)
            v_out[n, :, here] = (product + p_in[n, :, here].astype(F32)).astype(BF16)
            return 0

        lax.fori_loop(0, kb // vb, block, 0)

        @pl.when(n < chips - 1)
        def _():
            ws_copy(n + 1, 1).start()

    per_step = -(-chips // (STEPS - 1))

    def each_round(s, top, act):
        for i in range(per_step):
            n = s * per_step + i

            @pl.when((n >= 0) & (n < top))
            def _():
                act(n)

    def x_copy(s, h, j):
        q = tower_back(j)
        target = q * ratio + t // R
        m = lax.rem(t, R) * halves + h
        return target, remote(
            z_buf.at[s, h, q], x_buf.at[s, m], x_send.at[h, j], x_recv.at[s, m], "tp", target
        )

    def z_copy(s, h, j):
        return remote(
            z_buf.at[s, h, r],
            z_buf.at[s, h, r],
            z_send.at[h, j],
            z_recv.at[s, h, j],
            "rep",
            tower(j),
        )

    def z_arrival(s, h, j):
        q = tower_back(j)
        return remote(
            z_buf.at[s, h, q],
            z_buf.at[s, h, q],
            z_send.at[h, j],
            z_recv.at[s, h, j],
            "rep",
            tower(j),
        )

    def sq_copy(s, k):
        return remote(
            sq_out, sq_in.at[s, k], sq_send.at[k], sq_recv.at[s, k], "tp", plane(k)
        )

    def step(s, _):
        mixed = state[...] + emb_f[s]
        mixed = (mixed * gain_own).astype(BF16)
        for h in range(halves):
            z_buf[s, h, r] = mixed[:, h * hw : (h + 1) * hw]
        for h in range(halves):
            for j in range(1, R):
                z_copy(s, h, j).start()

        def forward(h, j):
            target, copy = x_copy(s, h, j)

            @pl.when(target != t)
            def _():
                copy.start()

            @pl.when(target == t)
            def _():
                x_buf[s, lax.rem(t, R) * halves + h] = z_buf[s, h, tower_back(j)]

        for h in range(halves):
            forward(h, 0)
        each_round(s - 1, chips - 1, lambda n: v_copy(n).start())
        each_round(s, chips, v_other)
        for h in range(halves):
            for j in range(1, R):
                z_arrival(s, h, j).wait_recv()
                forward(h, j)
        each_round(s, chips, v_own)

        for m in range(R):
            source = lax.rem(t, ratio) * R + m

            @pl.when(source != t)
            def _():
                for h in range(halves):
                    remote(
                        z_buf.at[s, h, 0],
                        x_buf.at[s, m * halves + h],
                        x_send.at[h, 0],
                        x_recv.at[s, m * halves + h],
                        "tp",
                        source,
                    ).wait_recv()

        x = jnp.concatenate([x_buf[s, m] for m in range(R * halves)], axis=1)
        plain = x.astype(F32) * gain_back
        plain = plain * plain
        lanes = plain[:, :128]
        for b in range(1, kb // 128):
            lanes = lanes + plain[:, b * 128 : (b + 1) * 128]
        sq_out[:, :rows] = lax.dot_general(
            jnp.ones((8, 128), F32),
            lanes,
            (((1,), (1,)), ((), ())),
            precision=EXACT,
            preferred_element_type=F32,
        )
        for k in range(1, T):
            sq_copy(s, k).start()
        sq_in[s, 0] = sq_out[...]

        def multiply(kk, _):
            k = T - 1 - kk
            product = jnp.dot(
                x, w_buf[:, cols(flip(t, k, T) * cw, cw)], preferred_element_type=F32
            ).astype(BF16)

            @pl.when(kk < T - 1)
            def _():
                rs_out[k] = product
                rs_copy(s + 1, k).start()

            @pl.when(kk == T - 1)
            def _():
                rs_in[s + 1, 0] = product

            return 0

        lax.fori_loop(0, T, multiply, 0)
        for k in range(1, T):
            sq_copy(s, k).wait_recv()
        squares = sq_in[s, 0]
        for k in range(1, T):
            squares = squares + sq_in[s, k]
        column = lax.dot_general(
            squares,
            jnp.full((8, 128), 0.125, F32),
            (((0,), (0,)), ((), ())),
            precision=EXACT,
            preferred_element_type=F32,
        )[:rows, :1]
        inverse = lax.rsqrt(column / width + 1e-05)
        update = finish(s + 1) * inverse
        state[...] += update / (1.0 + jnp.exp(-update))
        for k in range(1, T):
            sq_copy(s, k).wait_send()
        for h in range(halves):
            for j in range(1, R):
                z_copy(s, h, j).wait_send()
            for j in range(R):
                target, copy = x_copy(s, h, j)

                @pl.when(target != t)
                def _():
                    copy.wait_send()

        return 0

    sq_out[...] = jnp.zeros_like(sq_out)
    lax.fori_loop(0, STEPS, step, 0)

    def f_copy(k):
        return remote(f_out.at[k], f_in.at[t], f_send.at[k], f_recv.at[k], "tp", plane(k))

    blank = jnp.zeros((16 - own_rows, cw), F32)
    for k in range(T):
        here = pl.ds(pl.multiple_of(plane(k) * own_rows, own_rows), own_rows)
        f_out[k] = jnp.concatenate([state[here, :], blank], axis=0).astype(BF16)
        if k > 0:
            f_copy(k).start()
    f_in[t] = f_out[0]

    for k in range(1, T):
        remote(
            f_out.at[k],
            f_in.at[lax.rem(t - k + T, T)],
            f_send.at[k],
            f_recv.at[k],
            "tp",
            plane(k),
        ).wait()
    half = T // 2
    for k in range(half):
        top = f_in[k].astype(F32)[:own_rows]
        low = f_in[k + half].astype(F32)[:own_rows]
        g_buf[r, :, k * cw : (k + 1) * cw] = jnp.concatenate([top, low], axis=0).astype(BF16)

    def g_copy(j):
        return remote(g_buf.at[r], g_buf.at[r], g_send.at[j], g_recv.at[j], "rep", tower(j))

    for j in range(1, R):
        g_copy(j).start()

    def v_wait(n, _):
        v_copy(n).wait()
        return 0

    lax.fori_loop(0, chips - 1, v_wait, 0)

    def p_wait(n, _):
        p_copy(n).wait_send()
        return 0

    lax.fori_loop(0, chips, p_wait, 0)

    def v_sum(b, _):
        here = cols(b * vb, vb)
        total = v_out[chips - 1, :, here].astype(F32)
        for n in range(chips - 1):
            total = total + v_in[n, :, here].astype(F32)
        for n in range(rr):
            ver_ref[n, :, here] = (
                resid_ref[n, :, here].astype(F32)
                + total[n * draft_len : (n + 1) * draft_len]
            ).astype(BF16)
        return 0

    lax.fori_loop(0, kb // vb, v_sum, 0)

    for j in range(1, R):
        q = tower_back(j)
        remote(g_buf.at[q], g_buf.at[q], g_send.at[j], g_recv.at[j], "rep", tower(j)).wait()
    for q in range(R):
        block = g_buf[q].astype(F32)
        out_ref[:, q * nb : q * nb + nb // 2] = block[:own_rows].astype(BF16)
        out_ref[:, q * nb + nb // 2 : (q + 1) * nb] = block[own_rows:].astype(BF16)

    for j in range(1, R):
        a_copy(j).wait_send()

    @pl.when(home != r)
    def _():
        ra_copy().wait_send()

    for k in range(1, T):
        e_copy(k).wait_send()


def local(
    T,
    R,
    queries,
    kv_cache,
    kv_new,
    cache_len,
    out_proj,
    residual,
    accepted,
    draft_emb,
    draft_gain,
    draft_proj,
):
    row_count, draft_len, kdim = queries.shape
    width = draft_gain.shape[0]
    rows = row_count * R
    own_rows, steps = draft_emb.shape[:2]
    cw = width // (T * R)
    kb = width // T
    nb = width // R
    halves = 2 if cw >= 256 else 1
    emb = draft_emb.transpose(1, 0, 2).reshape(steps * own_rows, width)
    emb_rows = -(-steps * own_rows // 16) * 16
    emb = jnp.pad(emb, ((0, emb_rows - steps * own_rows), (0, 0)))
    token_rows = row_count * draft_len
    dma = pltpu.SemaphoreType.DMA
    vmem = pl.BlockSpec(memory_space=pltpu.VMEM)
    smem = pl.BlockSpec(memory_space=pltpu.SMEM)
    hbm = pl.BlockSpec(memory_space=pl.ANY)
    verified, features = pl.pallas_call(
        functools.partial(fused, T, R, steps),
        out_shape=(
            jax.ShapeDtypeStruct((row_count, draft_len, kb), BF16),
            jax.ShapeDtypeStruct((own_rows, width), BF16),
        ),
        in_specs=[smem] * 2 + [vmem] * 4 + [hbm] * 4,
        out_specs=(vmem, vmem),
        scratch_shapes=[
            pltpu.VMEM((row_count, 2, kv_cache.shape[2], HEAD_DIM), BF16),
            pltpu.VMEM((8 * row_count, kdim), F32),
            pltpu.VMEM((token_rows, kdim), BF16),
            pltpu.VMEM((row_count, kdim), BF16),
            pltpu.VMEM((row_count, kb), F32),
            pltpu.VMEM((row_count, kb), BF16),
            pltpu.VMEM((kb, nb), BF16),
            pltpu.VMEM((kdim, nb), BF16),
            pltpu.VMEM((2, kdim, kb), BF16),
            pltpu.VMEM((T, emb_rows, cw), BF16),
            pltpu.VMEM((steps, rows, cw), F32),
            pltpu.VMEM((R, row_count, kdim), BF16),
            pltpu.VMEM((R, row_count, kb), BF16),
            pltpu.VMEM((rows, cw), F32),
            pltpu.VMEM((rows, cw), F32),
            pltpu.VMEM((T, rows, cw), BF16),
            pltpu.VMEM((steps + 1, T, rows, cw), BF16),
            pltpu.VMEM((8, 128), F32),
            pltpu.VMEM((steps, T, 8, 128), F32),
            pltpu.VMEM((steps, halves, R, rows, cw // halves), BF16),
            pltpu.VMEM((steps, R * halves, rows, cw // halves), BF16),
            pltpu.VMEM((T, 16, cw), BF16),
            pltpu.VMEM((T, 16, cw), BF16),
            pltpu.VMEM((R, 16, nb // 2), BF16),
            pltpu.VMEM((T // 2, token_rows, kb), BF16),
            pltpu.VMEM((T // 2, token_rows, kb), BF16),
            pltpu.VMEM((T // 2, token_rows, kb), BF16),
            pltpu.VMEM((T // 2, token_rows, kb), BF16),
            dma,
            dma,
            dma,
            dma((2,)),
            dma((T,)),
            dma((T,)),
            dma((R,)),
            dma((R,)),
            dma,
            dma((R,)),
            dma((T,)),
            dma((steps + 1, T)),
            dma((T,)),
            dma((steps, T)),
            dma((halves, R)),
            dma((steps, halves, R)),
            dma((halves, R)),
            dma((steps, R * halves)),
            dma((T,)),
            dma((T,)),
            dma((R,)),
            dma((R,)),
            dma((T // 2,)),
            dma((T // 2,)),
            dma((T // 2,)),
            dma((T // 2,)),
        ],
        compiler_params=pltpu.CompilerParams(
            collective_id=0, has_side_effects=True, vmem_limit_bytes=56 * 2**20
        ),
        name="verify_and_draft",
    )(
        cache_len,
        accepted,
        queries,
        kv_new,
        residual,
        draft_gain.astype(F32).reshape(1, width),
        kv_cache,
        emb,
        out_proj,
        draft_proj,
    )
    return verified, features


def solution(mesh):
    in_specs = (
        P("rep", None, "tp"),
        P("rep", None, None, None),
        P("rep", None, None, None),
        P("rep"),
        P("tp", None),
        P("rep", None, "tp"),
        P("rep"),
        P("tp", None, None),
        P(),
        P("tp", "rep"),
    )
    out_specs = (P("rep", None, "tp"), P("tp", None))
    body = functools.partial(local, mesh.shape["tp"], mesh.shape["rep"])
    return jax.shard_map(body, mesh=mesh, in_specs=in_specs, out_specs=out_specs, check_vma=False)
```

```python
import functools

import jax
import jax.numpy as jnp
from jax import lax
from jax.experimental import pallas as pl
from jax.experimental.pallas import tpu as pltpu
from jax.sharding import PartitionSpec as P

KV_HEADS = 4
HEAD_DIM = 128
MESH = pl.DeviceIdType.MESH
F32 = jnp.float32
BF16 = jnp.bfloat16
EXACT = lax.Precision.HIGHEST


def fused(
    T,
    R,
    STEPS,
    len_ref,
    pick_ref,
    q_ref,
    fresh_ref,
    resid_ref,
    gain_ref,
    emb_raw,
    kv_ref,
    oproj_ref,
    dproj_ref,
    ver_ref,
    out_ref,
    kv_buf,
    padded,
    attn_ref,
    acc_ref,
    racc_ref,
    emb_ref,
    acc_f,
    w_buf,
    wo_buf,
    ws_buf,
    emb_in,
    emb_f,
    acc_in,
    racc_in,
    part,
    state,
    rs_out,
    rs_in,
    sq_out,
    sq_in,
    z_buf,
    x_buf,
    f_out,
    f_in,
    g_buf,
    p_out,
    p_in,
    v_out,
    v_in,
    kv_sem,
    w_sem,
    wo_sem,
    ws_sem,
    e_send,
    e_recv,
    a_send,
    a_recv,
    ra_send,
    ra_recv,
    rs_send,
    rs_recv,
    sq_send,
    sq_recv,
    z_send,
    z_recv,
    x_send,
    x_recv,
    f_send,
    f_recv,
    g_send,
    g_recv,
    p_send,
    p_recv,
    v_send,
    v_recv,
):
    t = lax.axis_index("tp")
    r = lax.axis_index("rep")
    ratio = T // R
    rows, cw = state.shape
    width = gain_ref.shape[1]
    kb = width // T
    nb = width // R
    own_rows = rows // T
    rr = acc_ref.shape[0]
    tokens, kdim = q_ref.shape
    draft_len = tokens // rr
    heads = kdim // HEAD_DIM
    chips = T // 2
    core = lax.rem(t, 2)
    chip = t // 2
    halves, hw = x_buf.shape[1] // R, x_buf.shape[3]

    def plane(k):
        return lax.rem(t + k, T)

    def flip(index, k, limit):
        out, bit = 0, 1
        while bit < limit:
            out = out + bit * lax.rem(index // bit + k // bit, 2)
            bit *= 2
        return out

    def tower(j):
        return lax.rem(r + j, R)

    def tower_back(j):
        return lax.rem(r - j + R, R)

    def remote(src, dst, send, recv, axis, index):
        return pltpu.make_async_remote_copy(
            src_ref=src,
            dst_ref=dst,
            send_sem=send,
            recv_sem=recv,
            device_id={axis: index},
            device_id_type=MESH,
        )

    def cols(start, size):
        return pl.ds(pl.multiple_of(start, 128), size)

    kv_group = t * heads // (heads * T // KV_HEADS)
    kv_copy = pltpu.make_async_copy(
        kv_ref.at[:, :, :, cols(kv_group * HEAD_DIM, HEAD_DIM)], kv_buf, kv_sem
    )
    kv_copy.start()
    wo_copy = pltpu.make_async_copy(oproj_ref.at[:, cols(r * nb, nb)], wo_buf, wo_sem)
    wo_copy.start()

    def turn(n, own):
        k = chips - 1 - n
        swapped = (k // 4) * 4 + lax.rem(k, 2) * 2 + lax.rem(k // 2, 2)
        return k + (core if own else 1 - core) * (swapped - k)

    def served(n, own):
        return flip(chip, turn(n, own), chips) * 2 + (core if own else 1 - core)

    def ws_copy(n, own):
        return pltpu.make_async_copy(
            oproj_ref.at[:, cols(served(n, own) * kb, kb)], ws_buf.at[own], ws_sem.at[own]
        )

    row_at = lax.broadcasted_iota(jnp.int32, (rr, 128), 0)
    picked = row_at * 0
    for n in range(rr):
        picked = jnp.where(row_at == n, pick_ref[n], picked)
    picked = picked[:, :1]
    chosen = jnp.zeros((rr, kb), F32)
    for i in range(draft_len):
        chosen = jnp.where(picked == i, resid_ref[i * rr : (i + 1) * rr, :].astype(F32), chosen)
    racc_ref[...] = chosen.astype(BF16)

    emb_rows = emb_ref.shape[0]
    emb_blank = jnp.zeros((emb_rows - emb_raw.shape[0], nb // 2), F32)

    def tile_up(b, _):
        here = cols(b * (nb // 2), nb // 2)
        emb_ref[:, here] = jnp.concatenate(
            [emb_raw[:, here].astype(F32), emb_blank], axis=0
        ).astype(BF16)
        return 0

    lax.fori_loop(0, 2 * R, tile_up, 0)

    barrier = pltpu.get_barrier_semaphore()
    for k in range(1, T):
        pl.semaphore_signal(barrier, inc=1, device_id={"tp": plane(k)}, device_id_type=MESH)
    for j in range(1, R):
        pl.semaphore_signal(barrier, inc=1, device_id={"rep": tower(j)}, device_id_type=MESH)
    pl.semaphore_wait(barrier, T - 1 + R - 1)

    home = t // ratio
    ra_offset = lax.rem(home - r + R, R)

    def ra_copy():
        return remote(racc_ref, racc_in.at[r], ra_send, ra_recv.at[ra_offset], "rep", home)

    @pl.when(home != r)
    def _():
        ra_copy().start()

    @pl.when(home == r)
    def _():
        racc_in[r] = racc_ref[...]

    w_copy = pltpu.make_async_copy(dproj_ref, w_buf, w_sem)
    w_copy.start()

    def e_copy(k):
        return remote(
            emb_ref.at[:, cols((r * T + plane(k)) * cw, cw)],
            emb_in.at[k],
            e_send.at[k],
            e_recv.at[k],
            "tp",
            plane(k),
        )

    e_own = pltpu.make_async_copy(
        emb_ref.at[:, cols((r * T + t) * cw, cw)], emb_in.at[0], e_send.at[0]
    )
    e_own.start()

    for k in range(1, T):
        e_copy(k).start()
    ws_copy(0, 0).start()
    ws_copy(0, 1).start()

    place_at = lax.broadcasted_iota(jnp.int32, (8 * rr, tokens), 0)
    token_at = lax.broadcasted_iota(jnp.int32, (8 * rr, tokens), 1)
    spread = (token_at == lax.rem(place_at, 8) * rr + place_at // 8) & (
        lax.rem(place_at, 8) < draft_len
    )
    padded[...] = jnp.dot(
        jnp.where(spread, 1.0, 0.0).astype(BF16), q_ref[...], preferred_element_type=F32
    )
    kv_copy.wait()
    tall = 8 * heads
    scale = HEAD_DIM ** (-0.5)
    token = lax.rem(lax.broadcasted_iota(jnp.int32, (tall, 128), 0), 8)
    fresh_ok = lax.broadcasted_iota(jnp.int32, (tall, 128), 1) <= token
    slots = kv_buf.shape[2]
    slot_at = lax.broadcasted_iota(jnp.int32, (tall, slots), 1)
    across = (((1,), (1,)), ((), ()))
    fresh_cols = cols(kv_group * HEAD_DIM, HEAD_DIM)
    unused = jnp.zeros((128 - draft_len, HEAD_DIM), F32)

    def attend_row(n, _):
        query = padded[pl.ds(pl.multiple_of(n * 8, 8), 8), :]
        query = jnp.concatenate(
            [query[:, h * HEAD_DIM : (h + 1) * HEAD_DIM] for h in range(heads)], axis=0
        ).astype(BF16)
        fresh_keys = jnp.concatenate(
            [fresh_ref[n, :, 0, fresh_cols].astype(F32), unused], axis=0
        ).astype(BF16)
        fresh_vals = jnp.concatenate(
            [fresh_ref[n, :, 1, fresh_cols].astype(F32), unused], axis=0
        ).astype(BF16)
        cache_scores = (
            lax.dot_general(query, kv_buf[n, 0], across, preferred_element_type=F32) * scale
        )
        fresh_scores = (
            lax.dot_general(query, fresh_keys, across, preferred_element_type=F32) * scale
        )
        cache_scores = jnp.where(slot_at < len_ref[n], cache_scores, -jnp.inf)
        fresh_scores = jnp.where(fresh_ok, fresh_scores, -jnp.inf)
        highest = jnp.maximum(
            jnp.max(cache_scores, axis=1, keepdims=True),
            jnp.max(fresh_scores, axis=1, keepdims=True),
        )
        cache_exp = jnp.exp(cache_scores - highest)
        fresh_exp = jnp.exp(fresh_scores - highest)
        total = jnp.sum(cache_exp, axis=1, keepdims=True) + jnp.sum(
            fresh_exp, axis=1, keepdims=True
        )
        mixed = jnp.dot(
            (cache_exp / total).astype(BF16), kv_buf[n, 1], preferred_element_type=F32
        ) + jnp.dot((fresh_exp / total).astype(BF16), fresh_vals, preferred_element_type=F32)
        padded[pl.ds(pl.multiple_of(n * 8, 8), 8), :] = jnp.concatenate(
            [mixed[h * 8 : (h + 1) * 8] for h in range(heads)], axis=1
        )
        return 0

    lax.fori_loop(0, rr, attend_row, 0, unroll=4)

    attended = padded[...].astype(BF16)
    row_at = lax.broadcasted_iota(jnp.int32, (rr, 8 * rr), 0)
    chosen = lax.broadcasted_iota(jnp.int32, (rr, 8 * rr), 1) == row_at * 8 + picked
    acc_ref[...] = jnp.dot(
        jnp.where(chosen, 1.0, 0.0).astype(BF16), attended, preferred_element_type=F32
    ).astype(BF16)

    def a_copy(j):
        return remote(acc_ref, acc_in.at[r], a_send.at[j], a_recv.at[j], "rep", tower(j))

    for j in range(1, R):
        a_copy(j).start()
    acc_in[r] = acc_ref[...]

    token_at = lax.broadcasted_iota(jnp.int32, (tokens, 8 * rr), 0)
    place_at = lax.broadcasted_iota(jnp.int32, (tokens, 8 * rr), 1)
    kept = (token_at == lax.rem(place_at, 8) * rr + place_at // 8) & (
        lax.rem(place_at, 8) < draft_len
    )
    attn_ref[...] = jnp.dot(
        jnp.where(kept, 1.0, 0.0).astype(BF16), attended, preferred_element_type=F32
    ).astype(BF16)


    for j in range(1, R):
        a_copy(j).wait_recv()

    @pl.when(home == r)
    def _():
        for j in range(1, R):
            remote(
                racc_ref, racc_in.at[tower_back(j)], ra_send, ra_recv.at[j], "rep", tower(j)
            ).wait_recv()

    wo_copy.wait()

    def rs_copy(i, k):
        return remote(
            rs_out.at[k], rs_in.at[i, k], rs_send.at[k], rs_recv.at[i, k], "tp", flip(t, k, T)
        )

    def finish(i):
        for k in range(1, T):
            rs_copy(i, k).wait_recv()
        total = rs_in[i, 0].astype(F32)
        for k in range(1, T):
            total = total + rs_in[i, k].astype(F32)
        for k in range(1, T):
            rs_copy(i, k).wait_send()
        return total

    first = acc_in[...].reshape(rows, acc_ref.shape[1])

    def project(kk, _):
        k = T - 1 - kk
        c = flip(t, k, T)
        part[...] = jnp.dot(first, wo_buf[:, cols(c * cw, cw)], preferred_element_type=F32)

        @pl.when(r * ratio + c // R == t)
        def _():
            part[...] += (
                racc_in[:, :, cols(lax.rem(c, R) * cw, cw)].reshape(rows, cw).astype(F32)
            )

        @pl.when(kk < T - 1)
        def _():
            rs_out[k] = part[...].astype(BF16)
            rs_copy(0, k).start()

        @pl.when(kk == T - 1)
        def _():
            rs_in[0, 0] = part[...].astype(BF16)

        return 0

    lax.fori_loop(0, T, project, 0)

    e_own.wait()
    for k in range(1, T):
        e_copy(k).wait_recv()

    def place(k, _):
        source = lax.rem(t - k + T, T)
        block = emb_in[k].astype(F32)
        for s in range(STEPS):
            emb_f[s, pl.ds(pl.multiple_of(source * own_rows, own_rows), own_rows), :] = block[
                s * own_rows : (s + 1) * own_rows
            ]
        return 0

    lax.fori_loop(0, T, place, 0)
    state[...] = finish(0).astype(BF16).astype(F32)
    w_copy.wait()

    gain_own = gain_ref[:, cols((r * T + t) * cw, cw)].astype(F32)
    gain_back = 1.0 / gain_ref[:, cols(t * kb, kb)].astype(F32)

    vb = min(kb, 512)

    def p_copy(n):
        return remote(
            p_out.at[n], p_in.at[n], p_send.at[n], p_recv.at[n], "tp", chip * 2 + 1 - core
        )

    def v_copy(n):
        return remote(
            v_out.at[n], v_in.at[n], v_send.at[n], v_recv.at[n], "tp", served(n, True)
        )

    def v_other(n):
        ws_copy(n, 0).wait()

        def block(b, _):
            here = cols(b * vb, vb)
            p_out[n, :, here] = jnp.dot(
                attn_ref[...], ws_buf[0, :, here], preferred_element_type=F32
            ).astype(BF16)
            return 0

        lax.fori_loop(0, kb // vb, block, 0)
        p_copy(n).start()

        @pl.when(n < chips - 1)
        def _():
            ws_copy(n + 1, 0).start()

    def v_own(n):
        ws_copy(n, 1).wait()
        p_copy(n).wait_recv()

        def block(b, _):
            here = cols(b * vb, vb)
            product = jnp.dot(attn_ref[...], ws_buf[1, :, here], preferred_element_type=F32)
            v_out[n, :, here] = (product + p_in[n, :, here].astype(F32)).astype(BF16)
            return 0

        lax.fori_loop(0, kb // vb, block, 0)

        @pl.when(n < chips - 1)
        def _():
            ws_copy(n + 1, 1).start()

    per_step = -(-chips // (STEPS - 1))

    def each_round(s, top, act):
        for i in range(per_step):
            n = s * per_step + i

            @pl.when((n >= 0) & (n < top))
            def _():
                act(n)

    def x_copy(s, h, j):
        q = tower_back(j)
        target = q * ratio + t // R
        m = lax.rem(t, R) * halves + h
        return target, remote(
            z_buf.at[s, h, q], x_buf.at[s, m], x_send.at[h, j], x_recv.at[s, m], "tp", target
        )

    def z_copy(s, h, j):
        return remote(
            z_buf.at[s, h, r],
            z_buf.at[s, h, r],
            z_send.at[h, j],
            z_recv.at[s, h, j],
            "rep",
            tower(j),
        )

    def z_arrival(s, h, j):
        q = tower_back(j)
        return remote(
            z_buf.at[s, h, q],
            z_buf.at[s, h, q],
            z_send.at[h, j],
            z_recv.at[s, h, j],
            "rep",
            tower(j),
        )

    def sq_copy(s, k):
        return remote(
            sq_out, sq_in.at[s, k], sq_send.at[k], sq_recv.at[s, k], "tp", plane(k)
        )

    def step(s, _):
        mixed = state[...] + emb_f[s]
        mixed = (mixed * gain_own).astype(BF16)
        for h in range(halves):
            z_buf[s, h, r] = mixed[:, h * hw : (h + 1) * hw]
        for h in range(halves):
            for j in range(1, R):
                z_copy(s, h, j).start()

        def forward(h, j):
            target, copy = x_copy(s, h, j)

            @pl.when(target != t)
            def _():
                copy.start()

            @pl.when(target == t)
            def _():
                x_buf[s, lax.rem(t, R) * halves + h] = z_buf[s, h, tower_back(j)]

        for h in range(halves):
            forward(h, 0)
        each_round(s - 1, chips - 1, lambda n: v_copy(n).start())
        each_round(s, chips, v_other)
        for h in range(halves):
            for j in range(1, R):
                z_arrival(s, h, j).wait_recv()
                forward(h, j)
            if h == 0:
                each_round(s, chips, v_own)

        def arrive(h):
            for m in range(R):
                source = lax.rem(t, ratio) * R + m

                @pl.when(source != t)
                def _():
                    remote(
                        z_buf.at[s, h, 0],
                        x_buf.at[s, m * halves + h],
                        x_send.at[h, 0],
                        x_recv.at[s, m * halves + h],
                        "tp",
                        source,
                    ).wait_recv()

        def product(h, other):
            here = cols(flip(chip, other, chips) * 2 * cw, 2 * cw)
            total = jnp.dot(
                x_buf[s, h], w_buf[h * hw : (h + 1) * hw, here], preferred_element_type=F32
            )
            for m in range(1, R):
                total = total + jnp.dot(
                    x_buf[s, m * halves + h],
                    w_buf[m * cw + h * hw : m * cw + (h + 1) * hw, here],
                    preferred_element_type=F32,
                )
            return total

        for h in range(halves - 1):
            arrive(h)

            def begin(n, _):
                other = chips - 1 - n
                total = product(h, other)
                acc_f[other] = total if h == 0 else acc_f[other] + total
                return 0

            lax.fori_loop(0, chips, begin, 0)
        arrive(halves - 1)

        def complete(n, _):
            other = chips - 1 - n
            total = product(halves - 1, other)
            if halves > 1:
                total = acc_f[other] + total
            total = total.astype(BF16)
            rs_out[2 * other + core] = total[:, :cw]
            rs_out[2 * other + 1 - core] = total[:, cw:]
            rs_copy(s + 1, 2 * other + 1).start()

            @pl.when(other > 0)
            def _():
                rs_copy(s + 1, 2 * other).start()

            return 0

        lax.fori_loop(0, chips // 2, complete, 0)
        lanes = jnp.zeros((rows, 128), F32)
        for m in range(R * halves):
            plain = x_buf[s, m].astype(F32) * gain_back[:, m * hw : (m + 1) * hw]
            plain = plain * plain
            for b in range(hw // 128):
                lanes = lanes + plain[:, b * 128 : (b + 1) * 128]
        sq_out[:, :rows] = lax.dot_general(
            jnp.ones((8, 128), F32),
            lanes,
            (((1,), (1,)), ((), ())),
            precision=EXACT,
            preferred_element_type=F32,
        )
        for k in range(1, T):
            sq_copy(s, k).start()
        sq_in[s, 0] = sq_out[...]
        lax.fori_loop(chips // 2, chips, complete, 0)
        rs_in[s + 1, 0] = rs_out[0]
        for k in range(1, T):
            sq_copy(s, k).wait_recv()
        squares = sq_in[s, 0]
        for k in range(1, T):
            squares = squares + sq_in[s, k]
        column = lax.dot_general(
            squares,
            jnp.full((8, 128), 0.125, F32),
            (((0,), (0,)), ((), ())),
            precision=EXACT,
            preferred_element_type=F32,
        )[:rows, :1]
        inverse = lax.rsqrt(column / width + 1e-05)
        update = finish(s + 1) * inverse
        state[...] += update / (1.0 + jnp.exp(-update))
        for k in range(1, T):
            sq_copy(s, k).wait_send()
        for h in range(halves):
            for j in range(1, R):
                z_copy(s, h, j).wait_send()
            for j in range(R):
                target, copy = x_copy(s, h, j)

                @pl.when(target != t)
                def _():
                    copy.wait_send()

        return 0

    sq_out[...] = jnp.zeros_like(sq_out)
    lax.fori_loop(0, STEPS, step, 0)

    def f_copy(k):
        return remote(f_out.at[k], f_in.at[t], f_send.at[k], f_recv.at[k], "tp", plane(k))

    blank = jnp.zeros((16 - own_rows, cw), F32)
    for k in range(T):
        here = pl.ds(pl.multiple_of(plane(k) * own_rows, own_rows), own_rows)
        f_out[k] = jnp.concatenate([state[here, :], blank], axis=0).astype(BF16)
        if k > 0:
            f_copy(k).start()
    f_in[t] = f_out[0]

    for k in range(1, T):
        remote(
            f_out.at[k],
            f_in.at[lax.rem(t - k + T, T)],
            f_send.at[k],
            f_recv.at[k],
            "tp",
            plane(k),
        ).wait()
    half = T // 2
    for k in range(half):
        top = f_in[k].astype(F32)[:own_rows]
        low = f_in[k + half].astype(F32)[:own_rows]
        g_buf[r, :, k * cw : (k + 1) * cw] = jnp.concatenate([top, low], axis=0).astype(BF16)

    def g_copy(j):
        return remote(g_buf.at[r], g_buf.at[r], g_send.at[j], g_recv.at[j], "rep", tower(j))

    for j in range(1, R):
        g_copy(j).start()

    def v_wait(n, _):
        v_copy(n).wait()
        return 0

    lax.fori_loop(0, chips - 1, v_wait, 0)

    def p_wait(n, _):
        p_copy(n).wait_send()
        return 0

    lax.fori_loop(0, chips, p_wait, 0)

    def v_sum(b, _):
        here = cols(b * vb, vb)
        total = v_out[chips - 1, :, here].astype(F32)
        for n in range(chips - 1):
            total = total + v_in[n, :, here].astype(F32)
        ver_ref[:, here] = (resid_ref[:, here].astype(F32) + total).astype(BF16)
        return 0

    lax.fori_loop(0, kb // vb, v_sum, 0)

    for j in range(1, R):
        q = tower_back(j)
        remote(g_buf.at[q], g_buf.at[q], g_send.at[j], g_recv.at[j], "rep", tower(j)).wait()
    for q in range(R):
        block = g_buf[q].astype(F32)
        out_ref[:, q * nb : q * nb + nb // 2] = block[:own_rows].astype(BF16)
        out_ref[:, q * nb + nb // 2 : (q + 1) * nb] = block[own_rows:].astype(BF16)

    for j in range(1, R):
        a_copy(j).wait_send()

    @pl.when(home != r)
    def _():
        ra_copy().wait_send()

    for k in range(1, T):
        e_copy(k).wait_send()


def local(
    T,
    R,
    queries,
    kv_cache,
    kv_new,
    cache_len,
    out_proj,
    residual,
    accepted,
    draft_emb,
    draft_gain,
    draft_proj,
):
    row_count, draft_len, kdim = queries.shape
    width = draft_gain.shape[0]
    rows = row_count * R
    own_rows, steps = draft_emb.shape[:2]
    cw = width // (T * R)
    kb = width // T
    nb = width // R
    halves = 2 if cw >= 256 else 1
    emb_rows = -(-steps * own_rows // 16) * 16
    token_rows = row_count * draft_len
    dma = pltpu.SemaphoreType.DMA
    vmem = pl.BlockSpec(memory_space=pltpu.VMEM)
    smem = pl.BlockSpec(memory_space=pltpu.SMEM)
    hbm = pl.BlockSpec(memory_space=pl.ANY)
    verified, features = pl.pallas_call(
        functools.partial(fused, T, R, steps),
        out_shape=(
            jax.ShapeDtypeStruct((token_rows, kb), BF16),
            jax.ShapeDtypeStruct((own_rows, width), BF16),
        ),
        in_specs=[smem] * 2 + [vmem] * 5 + [hbm] * 3,
        out_specs=(vmem, vmem),
        scratch_shapes=[
            pltpu.VMEM((row_count, 2, kv_cache.shape[2], HEAD_DIM), BF16),
            pltpu.VMEM((8 * row_count, kdim), F32),
            pltpu.VMEM((token_rows, kdim), BF16),
            pltpu.VMEM((row_count, kdim), BF16),
            pltpu.VMEM((row_count, kb), BF16),
            pltpu.VMEM((emb_rows, width), BF16),
            pltpu.VMEM((T // 2, rows, 2 * cw), F32),
            pltpu.VMEM((kb, nb), BF16),
            pltpu.VMEM((kdim, nb), BF16),
            pltpu.VMEM((2, kdim, kb), BF16),
            pltpu.VMEM((T, emb_rows, cw), BF16),
            pltpu.VMEM((steps, rows, cw), F32),
            pltpu.VMEM((R, row_count, kdim), BF16),
            pltpu.VMEM((R, row_count, kb), BF16),
            pltpu.VMEM((rows, cw), F32),
            pltpu.VMEM((rows, cw), F32),
            pltpu.VMEM((T, rows, cw), BF16),
            pltpu.VMEM((steps + 1, T, rows, cw), BF16),
            pltpu.VMEM((8, 128), F32),
            pltpu.VMEM((steps, T, 8, 128), F32),
            pltpu.VMEM((steps, halves, R, rows, cw // halves), BF16),
            pltpu.VMEM((steps, R * halves, rows, cw // halves), BF16),
            pltpu.VMEM((T, 16, cw), BF16),
            pltpu.VMEM((T, 16, cw), BF16),
            pltpu.VMEM((R, 16, nb // 2), BF16),
            pltpu.VMEM((T // 2, token_rows, kb), BF16),
            pltpu.VMEM((T // 2, token_rows, kb), BF16),
            pltpu.VMEM((T // 2, token_rows, kb), BF16),
            pltpu.VMEM((T // 2, token_rows, kb), BF16),
            dma,
            dma,
            dma,
            dma((2,)),
            dma((T,)),
            dma((T,)),
            dma((R,)),
            dma((R,)),
            dma,
            dma((R,)),
            dma((T,)),
            dma((steps + 1, T)),
            dma((T,)),
            dma((steps, T)),
            dma((halves, R)),
            dma((steps, halves, R)),
            dma((halves, R)),
            dma((steps, R * halves)),
            dma((T,)),
            dma((T,)),
            dma((R,)),
            dma((R,)),
            dma((T // 2,)),
            dma((T // 2,)),
            dma((T // 2,)),
            dma((T // 2,)),
        ],
        compiler_params=pltpu.CompilerParams(
            collective_id=0, has_side_effects=True, vmem_limit_bytes=56 * 2**20
        ),
        name="verify_and_draft",
    )(
        cache_len,
        accepted,
        queries.transpose(1, 0, 2).reshape(token_rows, kdim),
        kv_new.transpose(0, 2, 1, 3),
        residual.transpose(1, 0, 2).reshape(token_rows, kb),
        draft_gain.reshape(1, width),
        draft_emb.transpose(1, 0, 2).reshape(steps * own_rows, width),
        kv_cache,
        out_proj,
        draft_proj,
    )
    return verified.reshape(draft_len, row_count, kb).transpose(1, 0, 2), features


def solution(mesh):
    in_specs = (
        P("rep", None, "tp"),
        P("rep", None, None, None),
        P("rep", None, None, None),
        P("rep"),
        P("tp", None),
        P("rep", None, "tp"),
        P("rep"),
        P("tp", None, None),
        P(),
        P("tp", "rep"),
    )
    out_specs = (P("rep", None, "tp"), P("tp", None))
    body = functools.partial(local, mesh.shape["tp"], mesh.shape["rep"])
    return jax.shard_map(body, mesh=mesh, in_specs=in_specs, out_specs=out_specs, check_vma=False)
```

```python
import functools

import jax
import jax.numpy as jnp
from jax import lax
from jax.experimental import pallas as pl
from jax.experimental.pallas import tpu as pltpu
from jax.sharding import PartitionSpec as P

KV_HEADS = 4
HEAD_DIM = 128
MESH = pl.DeviceIdType.MESH
F32 = jnp.float32
BF16 = jnp.bfloat16
EXACT = lax.Precision.HIGHEST


def fused(
    T,
    R,
    STEPS,
    len_ref,
    pick_ref,
    q_ref,
    fresh_ref,
    resid_ref,
    gain_ref,
    emb_raw,
    kv_ref,
    oproj_ref,
    dproj_ref,
    ver_ref,
    out_ref,
    kv_buf,
    padded,
    attn_ref,
    acc_ref,
    racc_ref,
    emb_ref,
    w_buf,
    wo_buf,
    ws_buf,
    emb_in,
    emb_f,
    acc_in,
    racc_in,
    part,
    state,
    rs_out,
    rs_in,
    sq_out,
    sq_in,
    z_buf,
    x_buf,
    f_out,
    f_in,
    g_buf,
    p_out,
    p_in,
    v_out,
    v_in,
    kv_sem,
    w_sem,
    wo_sem,
    ws_sem,
    e_send,
    e_recv,
    a_send,
    a_recv,
    ra_send,
    ra_recv,
    rs_send,
    rs_recv,
    sq_send,
    sq_recv,
    z_send,
    z_recv,
    x_send,
    x_recv,
    f_send,
    f_recv,
    g_send,
    g_recv,
    p_send,
    p_recv,
    v_send,
    v_recv,
):
    t = lax.axis_index("tp")
    r = lax.axis_index("rep")
    ratio = T // R
    rows, cw = state.shape
    width = gain_ref.shape[1]
    kb = width // T
    nb = width // R
    own_rows = rows // T
    rr = acc_ref.shape[0]
    tokens, kdim = q_ref.shape
    draft_len = tokens // rr
    heads = kdim // HEAD_DIM
    chips = T // 2
    core = lax.rem(t, 2)
    chip = t // 2
    halves, hw = z_buf.shape[1], z_buf.shape[4]

    def plane(k):
        return lax.rem(t + k, T)

    def flip(index, k, limit):
        out, bit = 0, 1
        while bit < limit:
            out = out + bit * lax.rem(index // bit + k // bit, 2)
            bit *= 2
        return out

    def tower(j):
        return lax.rem(r + j, R)

    def tower_back(j):
        return lax.rem(r - j + R, R)

    def remote(src, dst, send, recv, axis, index):
        return pltpu.make_async_remote_copy(
            src_ref=src,
            dst_ref=dst,
            send_sem=send,
            recv_sem=recv,
            device_id={axis: index},
            device_id_type=MESH,
        )

    def cols(start, size):
        return pl.ds(pl.multiple_of(start, 128), size)

    kv_group = t * heads // (heads * T // KV_HEADS)
    kv_copy = pltpu.make_async_copy(
        kv_ref.at[:, :, :, cols(kv_group * HEAD_DIM, HEAD_DIM)], kv_buf, kv_sem
    )
    kv_copy.start()
    wo_copy = pltpu.make_async_copy(oproj_ref.at[:, cols(r * nb, nb)], wo_buf, wo_sem)
    wo_copy.start()

    def turn(n, own):
        k = chips - 1 - n
        swapped = (k // 4) * 4 + lax.rem(k, 2) * 2 + lax.rem(k // 2, 2)
        return k + (core if own else 1 - core) * (swapped - k)

    def served(n, own):
        return flip(chip, turn(n, own), chips) * 2 + (core if own else 1 - core)

    def ws_copy(n, own):
        return pltpu.make_async_copy(
            oproj_ref.at[:, cols(served(n, own) * kb, kb)], ws_buf.at[own], ws_sem.at[own]
        )

    row_at = lax.broadcasted_iota(jnp.int32, (rr, 128), 0)
    picked = row_at * 0
    for n in range(rr):
        picked = jnp.where(row_at == n, pick_ref[n], picked)
    picked = picked[:, :1]
    chosen = jnp.zeros((rr, kb), F32)
    for i in range(draft_len):
        chosen = jnp.where(picked == i, resid_ref[i * rr : (i + 1) * rr, :].astype(F32), chosen)
    racc_ref[...] = chosen.astype(BF16)

    barrier = pltpu.get_barrier_semaphore()
    for k in range(1, T):
        pl.semaphore_signal(barrier, inc=1, device_id={"tp": plane(k)}, device_id_type=MESH)
    for j in range(1, R):
        pl.semaphore_signal(barrier, inc=1, device_id={"rep": tower(j)}, device_id_type=MESH)
    pl.semaphore_wait(barrier, T - 1 + R - 1)

    home = t // ratio
    ra_offset = lax.rem(home - r + R, R)

    def ra_copy():
        return remote(racc_ref, racc_in.at[r], ra_send, ra_recv.at[ra_offset], "rep", home)

    @pl.when(home != r)
    def _():
        ra_copy().start()

    @pl.when(home == r)
    def _():
        racc_in[r] = racc_ref[...]

    w_copy = pltpu.make_async_copy(dproj_ref, w_buf, w_sem)
    w_copy.start()

    ws_copy(0, 0).start()
    ws_copy(0, 1).start()

    place_at = lax.broadcasted_iota(jnp.int32, (8 * rr, tokens), 0)
    token_at = lax.broadcasted_iota(jnp.int32, (8 * rr, tokens), 1)
    spread = (token_at == lax.rem(place_at, 8) * rr + place_at // 8) & (
        lax.rem(place_at, 8) < draft_len
    )
    padded[...] = jnp.dot(
        jnp.where(spread, 1.0, 0.0).astype(BF16), q_ref[...], preferred_element_type=F32
    )
    kv_copy.wait()
    tall = 8 * heads
    scale = HEAD_DIM ** (-0.5)
    token = lax.rem(lax.broadcasted_iota(jnp.int32, (tall, 128), 0), 8)
    fresh_ok = lax.broadcasted_iota(jnp.int32, (tall, 128), 1) <= token
    slots = kv_buf.shape[2]
    slot_at = lax.broadcasted_iota(jnp.int32, (tall, slots), 1)
    across = (((1,), (1,)), ((), ()))
    fresh_cols = cols(kv_group * HEAD_DIM, HEAD_DIM)
    unused = jnp.zeros((128 - draft_len, HEAD_DIM), F32)

    def attend_row(n, _):
        query = padded[pl.ds(pl.multiple_of(n * 8, 8), 8), :]
        query = jnp.concatenate(
            [query[:, h * HEAD_DIM : (h + 1) * HEAD_DIM] for h in range(heads)], axis=0
        ).astype(BF16)
        fresh_keys = jnp.concatenate(
            [fresh_ref[n, :, 0, fresh_cols].astype(F32), unused], axis=0
        ).astype(BF16)
        fresh_vals = jnp.concatenate(
            [fresh_ref[n, :, 1, fresh_cols].astype(F32), unused], axis=0
        ).astype(BF16)
        cache_scores = (
            lax.dot_general(query, kv_buf[n, 0], across, preferred_element_type=F32) * scale
        )
        fresh_scores = (
            lax.dot_general(query, fresh_keys, across, preferred_element_type=F32) * scale
        )
        cache_scores = jnp.where(slot_at < len_ref[n], cache_scores, -jnp.inf)
        fresh_scores = jnp.where(fresh_ok, fresh_scores, -jnp.inf)
        highest = jnp.maximum(
            jnp.max(cache_scores, axis=1, keepdims=True),
            jnp.max(fresh_scores, axis=1, keepdims=True),
        )
        cache_exp = jnp.exp(cache_scores - highest)
        fresh_exp = jnp.exp(fresh_scores - highest)
        total = jnp.sum(cache_exp, axis=1, keepdims=True) + jnp.sum(
            fresh_exp, axis=1, keepdims=True
        )
        mixed = jnp.dot(
            (cache_exp / total).astype(BF16), kv_buf[n, 1], preferred_element_type=F32
        ) + jnp.dot((fresh_exp / total).astype(BF16), fresh_vals, preferred_element_type=F32)
        padded[pl.ds(pl.multiple_of(n * 8, 8), 8), :] = jnp.concatenate(
            [mixed[h * 8 : (h + 1) * 8] for h in range(heads)], axis=1
        )
        return 0

    lax.fori_loop(0, rr, attend_row, 0, unroll=4)

    attended = padded[...].astype(BF16)
    row_at = lax.broadcasted_iota(jnp.int32, (rr, 8 * rr), 0)
    chosen = lax.broadcasted_iota(jnp.int32, (rr, 8 * rr), 1) == row_at * 8 + picked
    acc_ref[...] = jnp.dot(
        jnp.where(chosen, 1.0, 0.0).astype(BF16), attended, preferred_element_type=F32
    ).astype(BF16)

    def a_copy(j):
        return remote(acc_ref, acc_in.at[r], a_send.at[j], a_recv.at[j], "rep", tower(j))

    for j in range(1, R):
        a_copy(j).start()
    acc_in[r] = acc_ref[...]

    emb_rows = emb_ref.shape[0]
    emb_blank = jnp.zeros((emb_rows - emb_raw.shape[0], nb // 2), F32)

    def tile_up(b, _):
        here = cols(b * (nb // 2), nb // 2)
        emb_ref[:, here] = jnp.concatenate(
            [emb_raw[:, here].astype(F32), emb_blank], axis=0
        ).astype(BF16)
        return 0

    lax.fori_loop(0, 2 * R, tile_up, 0)

    def e_copy(k):
        return remote(
            emb_ref.at[:, cols((r * T + plane(k)) * cw, cw)],
            emb_in.at[k],
            e_send.at[k],
            e_recv.at[k],
            "tp",
            plane(k),
        )

    e_own = pltpu.make_async_copy(
        emb_ref.at[:, cols((r * T + t) * cw, cw)], emb_in.at[0], e_send.at[0]
    )
    e_own.start()

    for k in range(1, T):
        e_copy(k).start()
    token_at = lax.broadcasted_iota(jnp.int32, (tokens, 8 * rr), 0)
    place_at = lax.broadcasted_iota(jnp.int32, (tokens, 8 * rr), 1)
    kept = (token_at == lax.rem(place_at, 8) * rr + place_at // 8) & (
        lax.rem(place_at, 8) < draft_len
    )
    attn_ref[...] = jnp.dot(
        jnp.where(kept, 1.0, 0.0).astype(BF16), attended, preferred_element_type=F32
    ).astype(BF16)


    for j in range(1, R):
        a_copy(j).wait_recv()

    @pl.when(home == r)
    def _():
        for j in range(1, R):
            remote(
                racc_ref, racc_in.at[tower_back(j)], ra_send, ra_recv.at[j], "rep", tower(j)
            ).wait_recv()

    wo_copy.wait()

    def rs_copy(i, k):
        return remote(
            rs_out.at[k], rs_in.at[i, k], rs_send.at[i, k], rs_recv.at[i, k], "tp", flip(t, k, T)
        )

    def finish(i):
        for k in range(1, T):
            rs_copy(i, k).wait_recv()
        total = rs_in[i, 0].astype(F32)
        for k in range(1, T):
            total = total + rs_in[i, k].astype(F32)
        return total

    def drain_sums(i):
        for k in range(1, T):
            rs_copy(i, k).wait_send()

    first = acc_in[...].reshape(rows, acc_ref.shape[1])

    def project(kk, _):
        k = T - 1 - kk
        c = flip(t, k, T)
        part[...] = jnp.dot(first, wo_buf[:, cols(c * cw, cw)], preferred_element_type=F32)

        @pl.when(r * ratio + c // R == t)
        def _():
            part[...] += (
                racc_in[:, :, cols(lax.rem(c, R) * cw, cw)].reshape(rows, cw).astype(F32)
            )

        @pl.when(kk < T - 1)
        def _():
            rs_out[k] = part[...].astype(BF16)
            rs_copy(0, k).start()

        @pl.when(kk == T - 1)
        def _():
            rs_in[0, 0] = part[...].astype(BF16)

        return 0

    lax.fori_loop(0, T, project, 0)

    e_own.wait()
    for k in range(1, T):
        e_copy(k).wait_recv()

    def place(k, _):
        source = lax.rem(t - k + T, T)
        block = emb_in[k].astype(F32)
        for s in range(STEPS):
            emb_f[s, pl.ds(pl.multiple_of(source * own_rows, own_rows), own_rows), :] = block[
                s * own_rows : (s + 1) * own_rows
            ]
        return 0

    lax.fori_loop(0, T, place, 0)
    state[...] = finish(0).astype(BF16).astype(F32)
    w_copy.wait()

    gain_own = gain_ref[:, cols((r * T + t) * cw, cw)].astype(F32)
    gain_back = 1.0 / gain_ref[:, cols(t * kb, kb)].astype(F32)

    vb = min(kb, 512)

    def p_copy(n):
        return remote(
            p_out.at[n], p_in.at[n], p_send.at[n], p_recv.at[n], "tp", chip * 2 + 1 - core
        )

    def v_copy(n):
        return remote(
            v_out.at[n], v_in.at[n], v_send.at[n], v_recv.at[n], "tp", served(n, True)
        )

    def v_other(n):
        ws_copy(n, 0).wait()

        def block(b, _):
            here = cols(b * vb, vb)
            p_out[n, :, here] = jnp.dot(
                attn_ref[...], ws_buf[0, :, here], preferred_element_type=F32
            ).astype(BF16)
            return 0

        lax.fori_loop(0, kb // vb, block, 0)
        p_copy(n).start()

        @pl.when(n < chips - 1)
        def _():
            ws_copy(n + 1, 0).start()

    def v_own(n):
        ws_copy(n, 1).wait()
        p_copy(n).wait_recv()

        def block(b, _):
            here = cols(b * vb, vb)
            product = jnp.dot(attn_ref[...], ws_buf[1, :, here], preferred_element_type=F32)
            v_out[n, :, here] = (product + p_in[n, :, here].astype(F32)).astype(BF16)
            return 0

        lax.fori_loop(0, kb // vb, block, 0)

        @pl.when(n < chips - 1)
        def _():
            ws_copy(n + 1, 1).start()

    per_step = -(-chips // (STEPS - 1))

    def each_round(s, top, act):
        for i in range(per_step):
            n = s * per_step + i

            @pl.when((n >= 0) & (n < top))
            def _():
                act(n)

    def x_place(s, m, h):
        return x_buf.at[s, :, cols(m * cw + h * hw, hw)]

    def x_copy(s, h, j):
        q = tower_back(j)
        target = q * ratio + t // R
        m = lax.rem(t, R)
        return target, remote(
            z_buf.at[s, h, q],
            x_place(s, m, h),
            x_send.at[s, h, j],
            x_recv.at[s, m * halves + h],
            "tp",
            target,
        )

    def z_copy(s, h, j):
        return remote(
            z_buf.at[s, h, r],
            z_buf.at[s, h, r],
            z_send.at[s, h, j],
            z_recv.at[s, h, j],
            "rep",
            tower(j),
        )

    def z_arrival(s, h, j):
        q = tower_back(j)
        return remote(
            z_buf.at[s, h, q],
            z_buf.at[s, h, q],
            z_send.at[s, h, j],
            z_recv.at[s, h, j],
            "rep",
            tower(j),
        )

    def sq_copy(s, k):
        return remote(
            sq_out, sq_in.at[s, k], sq_send.at[s, k], sq_recv.at[s, k], "tp", plane(k)
        )

    def drain(s):
        for k in range(1, T):
            sq_copy(s, k).wait_send()
        for h in range(halves):
            for j in range(1, R):
                z_copy(s, h, j).wait_send()
            for j in range(R):
                target, copy = x_copy(s, h, j)

                @pl.when(target != t)
                def _():
                    copy.wait_send()

    def step(s, _):
        mixed = state[...] + emb_f[s]
        mixed = (mixed * gain_own).astype(BF16)
        for h in range(halves):
            z_buf[s, h, r] = mixed[:, h * hw : (h + 1) * hw]
        for h in range(halves):
            for j in range(1, R):
                z_copy(s, h, j).start()

        def forward(h, j):
            target, copy = x_copy(s, h, j)

            @pl.when(target != t)
            def _():
                copy.start()

            @pl.when(target == t)
            def _():
                x_buf[s, :, cols(lax.rem(t, R) * cw + h * hw, hw)] = z_buf[
                    s, h, tower_back(j)
                ]

        for h in range(halves):
            forward(h, 0)
        each_round(s - 1, chips - 1, lambda n: v_copy(n).start())
        drain_sums(s)

        @pl.when(s > 0)
        def _():
            drain(s - 1)

        each_round(s, chips, v_other)
        for h in range(halves):
            for j in range(1, R):
                z_arrival(s, h, j).wait_recv()
                forward(h, j)
        each_round(s, chips, v_own)

        for m in range(R):
            source = lax.rem(t, ratio) * R + m

            @pl.when(source != t)
            def _():
                for h in range(halves):
                    remote(
                        z_buf.at[s, h, 0],
                        x_place(s, m, h),
                        x_send.at[s, h, 0],
                        x_recv.at[s, m * halves + h],
                        "tp",
                        source,
                    ).wait_recv()

        def multiply(n, _):
            other = chips - 1 - n
            start = flip(chip, other, chips) * 2 * cw
            for b in range(2):
                rs_out[2 * other + (1 - core if b else core)] = jnp.dot(
                    x_buf[s], w_buf[:, cols(start + b * cw, cw)], preferred_element_type=F32
                ).astype(BF16)
            rs_copy(s + 1, 2 * other + 1).start()

            @pl.when(other > 0)
            def _():
                rs_copy(s + 1, 2 * other).start()

            return 0

        lax.fori_loop(0, chips // 2, multiply, 0)
        lanes = jnp.zeros((rows, 128), F32)
        for b in range(kb // 128):
            here = slice(b * 128, (b + 1) * 128)
            plain = x_buf[s, :, here].astype(F32) * gain_back[:, here]
            lanes = lanes + plain * plain
        sq_out[:, :rows] = lax.dot_general(
            jnp.ones((8, 128), F32),
            lanes,
            (((1,), (1,)), ((), ())),
            precision=EXACT,
            preferred_element_type=F32,
        )
        for k in range(1, T):
            sq_copy(s, k).start()
        sq_in[s, 0] = sq_out[...]
        lax.fori_loop(chips // 2, chips, multiply, 0)
        rs_in[s + 1, 0] = rs_out[0]
        for k in range(1, T):
            sq_copy(s, k).wait_recv()
        squares = sq_in[s, 0]
        for k in range(1, T):
            squares = squares + sq_in[s, k]
        column = lax.dot_general(
            squares,
            jnp.full((8, 128), 0.125, F32),
            (((0,), (0,)), ((), ())),
            precision=EXACT,
            preferred_element_type=F32,
        )[:rows, :1]
        inverse = lax.rsqrt(column / width + 1e-05)
        update = finish(s + 1) * inverse
        state[...] += update / (1.0 + jnp.exp(-update))
        return 0

    sq_out[...] = jnp.zeros_like(sq_out)
    lax.fori_loop(0, STEPS, step, 0)
    drain_sums(STEPS)
    drain(STEPS - 1)

    def f_copy(k):
        return remote(f_out.at[k], f_in.at[t], f_send.at[k], f_recv.at[k], "tp", plane(k))

    blank = jnp.zeros((16 - own_rows, cw), F32)
    for k in range(T):
        here = pl.ds(pl.multiple_of(plane(k) * own_rows, own_rows), own_rows)
        f_out[k] = jnp.concatenate([state[here, :], blank], axis=0).astype(BF16)
        if k > 0:
            f_copy(k).start()
    f_in[t] = f_out[0]

    for k in range(1, T):
        remote(
            f_out.at[k],
            f_in.at[lax.rem(t - k + T, T)],
            f_send.at[k],
            f_recv.at[k],
            "tp",
            plane(k),
        ).wait()
    half = T // 2
    for k in range(half):
        top = f_in[k].astype(F32)[:own_rows]
        low = f_in[k + half].astype(F32)[:own_rows]
        g_buf[r, :, k * cw : (k + 1) * cw] = jnp.concatenate([top, low], axis=0).astype(BF16)

    def g_copy(j):
        return remote(g_buf.at[r], g_buf.at[r], g_send.at[j], g_recv.at[j], "rep", tower(j))

    for j in range(1, R):
        g_copy(j).start()

    def v_wait(n, _):
        v_copy(n).wait()
        return 0

    lax.fori_loop(0, chips - 1, v_wait, 0)

    def p_wait(n, _):
        p_copy(n).wait_send()
        return 0

    lax.fori_loop(0, chips, p_wait, 0)

    def v_sum(b, _):
        here = cols(b * vb, vb)
        total = v_out[chips - 1, :, here].astype(F32)
        for n in range(chips - 1):
            total = total + v_in[n, :, here].astype(F32)
        ver_ref[:, here] = (resid_ref[:, here].astype(F32) + total).astype(BF16)
        return 0

    lax.fori_loop(0, kb // vb, v_sum, 0)

    for j in range(1, R):
        q = tower_back(j)
        remote(g_buf.at[q], g_buf.at[q], g_send.at[j], g_recv.at[j], "rep", tower(j)).wait()
    for q in range(R):
        block = g_buf[q].astype(F32)
        out_ref[:, q * nb : q * nb + nb // 2] = block[:own_rows].astype(BF16)
        out_ref[:, q * nb + nb // 2 : (q + 1) * nb] = block[own_rows:].astype(BF16)

    for j in range(1, R):
        a_copy(j).wait_send()

    @pl.when(home != r)
    def _():
        ra_copy().wait_send()

    for k in range(1, T):
        e_copy(k).wait_send()


def local(
    T,
    R,
    queries,
    kv_cache,
    kv_new,
    cache_len,
    out_proj,
    residual,
    accepted,
    draft_emb,
    draft_gain,
    draft_proj,
):
    row_count, draft_len, kdim = queries.shape
    width = draft_gain.shape[0]
    rows = row_count * R
    own_rows, steps = draft_emb.shape[:2]
    cw = width // (T * R)
    kb = width // T
    nb = width // R
    halves = 2 if cw >= 256 else 1
    emb_rows = -(-steps * own_rows // 16) * 16
    token_rows = row_count * draft_len
    dma = pltpu.SemaphoreType.DMA
    vmem = pl.BlockSpec(memory_space=pltpu.VMEM)
    smem = pl.BlockSpec(memory_space=pltpu.SMEM)
    hbm = pl.BlockSpec(memory_space=pl.ANY)
    verified, features = pl.pallas_call(
        functools.partial(fused, T, R, steps),
        out_shape=(
            jax.ShapeDtypeStruct((token_rows, kb), BF16),
            jax.ShapeDtypeStruct((own_rows, width), BF16),
        ),
        in_specs=[smem] * 2 + [vmem] * 5 + [hbm] * 3,
        out_specs=(vmem, vmem),
        scratch_shapes=[
            pltpu.VMEM((row_count, 2, kv_cache.shape[2], HEAD_DIM), BF16),
            pltpu.VMEM((8 * row_count, kdim), F32),
            pltpu.VMEM((token_rows, kdim), BF16),
            pltpu.VMEM((row_count, kdim), BF16),
            pltpu.VMEM((row_count, kb), BF16),
            pltpu.VMEM((emb_rows, width), BF16),
            pltpu.VMEM((kb, nb), BF16),
            pltpu.VMEM((kdim, nb), BF16),
            pltpu.VMEM((2, kdim, kb), BF16),
            pltpu.VMEM((T, emb_rows, cw), BF16),
            pltpu.VMEM((steps, rows, cw), F32),
            pltpu.VMEM((R, row_count, kdim), BF16),
            pltpu.VMEM((R, row_count, kb), BF16),
            pltpu.VMEM((rows, cw), F32),
            pltpu.VMEM((rows, cw), F32),
            pltpu.VMEM((T, rows, cw), BF16),
            pltpu.VMEM((steps + 1, T, rows, cw), BF16),
            pltpu.VMEM((8, 128), F32),
            pltpu.VMEM((steps, T, 8, 128), F32),
            pltpu.VMEM((steps, halves, R, rows, cw // halves), BF16),
            pltpu.VMEM((steps, rows, kb), BF16),
            pltpu.VMEM((T, 16, cw), BF16),
            pltpu.VMEM((T, 16, cw), BF16),
            pltpu.VMEM((R, 16, nb // 2), BF16),
            pltpu.VMEM((T // 2, token_rows, kb), BF16),
            pltpu.VMEM((T // 2, token_rows, kb), BF16),
            pltpu.VMEM((T // 2, token_rows, kb), BF16),
            pltpu.VMEM((T // 2, token_rows, kb), BF16),
            dma,
            dma,
            dma,
            dma((2,)),
            dma((T,)),
            dma((T,)),
            dma((R,)),
            dma((R,)),
            dma,
            dma((R,)),
            dma((steps + 1, T)),
            dma((steps + 1, T)),
            dma((steps, T)),
            dma((steps, T)),
            dma((steps, halves, R)),
            dma((steps, halves, R)),
            dma((steps, halves, R)),
            dma((steps, R * halves)),
            dma((T,)),
            dma((T,)),
            dma((R,)),
            dma((R,)),
            dma((T // 2,)),
            dma((T // 2,)),
            dma((T // 2,)),
            dma((T // 2,)),
        ],
        compiler_params=pltpu.CompilerParams(
            collective_id=0, has_side_effects=True, vmem_limit_bytes=56 * 2**20
        ),
        name="verify_and_draft",
    )(
        cache_len,
        accepted,
        queries.transpose(1, 0, 2).reshape(token_rows, kdim),
        kv_new.transpose(0, 2, 1, 3),
        residual.transpose(1, 0, 2).reshape(token_rows, kb),
        draft_gain.reshape(1, width),
        draft_emb.transpose(1, 0, 2).reshape(steps * own_rows, width),
        kv_cache,
        out_proj,
        draft_proj,
    )
    return verified.reshape(draft_len, row_count, kb).transpose(1, 0, 2), features


def solution(mesh):
    in_specs = (
        P("rep", None, "tp"),
        P("rep", None, None, None),
        P("rep", None, None, None),
        P("rep"),
        P("tp", None),
        P("rep", None, "tp"),
        P("rep"),
        P("tp", None, None),
        P(),
        P("tp", "rep"),
    )
    out_specs = (P("rep", None, "tp"), P("tp", None))
    body = functools.partial(local, mesh.shape["tp"], mesh.shape["rep"])
    return jax.shard_map(body, mesh=mesh, in_specs=in_specs, out_specs=out_specs, check_vma=False)
```

```python
import functools

import jax
import jax.numpy as jnp
from jax import lax
from jax.experimental import pallas as pl
from jax.experimental.pallas import tpu as pltpu
from jax.sharding import PartitionSpec as P

KV_HEADS = 4
HEAD_DIM = 128
MESH = pl.DeviceIdType.MESH
F32 = jnp.float32
BF16 = jnp.bfloat16
EXACT = lax.Precision.HIGHEST


def fused(
    T,
    R,
    STEPS,
    len_ref,
    pick_ref,
    q_ref,
    fresh_ref,
    resid_ref,
    gain_ref,
    emb_raw,
    kv_ref,
    oproj_ref,
    dproj_ref,
    ver_ref,
    out_ref,
    kv_buf,
    padded,
    attn_ref,
    acc_ref,
    racc_ref,
    emb_ref,
    w_buf,
    wo_buf,
    ws_buf,
    emb_in,
    emb_f,
    acc_in,
    racc_in,
    part,
    state,
    q_out,
    q_in,
    rs_out,
    rs_in,
    sq_out,
    sq_in,
    z_buf,
    x_buf,
    f_out,
    f_in,
    g_buf,
    p_out,
    p_in,
    v_out,
    v_in,
    kv_sem,
    w_sem,
    wo_sem,
    ws_sem,
    e_send,
    e_recv,
    a_send,
    a_recv,
    ra_send,
    ra_recv,
    q_send,
    q_recv,
    rs_send,
    rs_recv,
    sq_send,
    sq_recv,
    z_send,
    z_recv,
    x_send,
    x_recv,
    f_send,
    f_recv,
    g_send,
    g_recv,
    p_send,
    p_recv,
    v_send,
    v_recv,
):
    t = lax.axis_index("tp")
    r = lax.axis_index("rep")
    ratio = T // R
    rows, cw = state.shape
    width = gain_ref.shape[1]
    kb = width // T
    nb = width // R
    own_rows = rows // T
    rr = acc_ref.shape[0]
    tokens, kdim = q_ref.shape
    draft_len = tokens // rr
    heads = kdim // HEAD_DIM
    chips = T // 2
    core = lax.rem(t, 2)
    chip = t // 2
    halves, hw = z_buf.shape[1], z_buf.shape[4]

    def plane(k):
        return lax.rem(t + k, T)

    def flip(index, k, limit):
        out, bit = 0, 1
        while bit < limit:
            out = out + bit * lax.rem(index // bit + k // bit, 2)
            bit *= 2
        return out

    def tower(j):
        return lax.rem(r + j, R)

    def tower_back(j):
        return lax.rem(r - j + R, R)

    def remote(src, dst, send, recv, axis, index):
        return pltpu.make_async_remote_copy(
            src_ref=src,
            dst_ref=dst,
            send_sem=send,
            recv_sem=recv,
            device_id={axis: index},
            device_id_type=MESH,
        )

    def cols(start, size):
        return pl.ds(pl.multiple_of(start, 128), size)

    kv_group = t * heads // (heads * T // KV_HEADS)
    kv_copy = pltpu.make_async_copy(
        kv_ref.at[:, :, :, cols(kv_group * HEAD_DIM, HEAD_DIM)], kv_buf, kv_sem
    )
    kv_copy.start()
    wo_copy = pltpu.make_async_copy(oproj_ref.at[:, cols(r * nb, nb)], wo_buf, wo_sem)
    wo_copy.start()

    def turn(n, own):
        k = chips - 1 - n
        swapped = (k // 4) * 4 + lax.rem(k, 2) * 2 + lax.rem(k // 2, 2)
        return k + (core if own else 1 - core) * (swapped - k)

    def served(n, own):
        return flip(chip, turn(n, own), chips) * 2 + (core if own else 1 - core)

    def ws_copy(n, own):
        return pltpu.make_async_copy(
            oproj_ref.at[:, cols(served(n, own) * kb, kb)], ws_buf.at[own], ws_sem.at[own]
        )

    barrier = pltpu.get_barrier_semaphore()
    for k in range(1, T):
        pl.semaphore_signal(barrier, inc=1, device_id={"tp": plane(k)}, device_id_type=MESH)
    for j in range(1, R):
        pl.semaphore_signal(barrier, inc=1, device_id={"rep": tower(j)}, device_id_type=MESH)
    pl.semaphore_wait(barrier, T - 1 + R - 1)

    straight = emb_raw.shape[0] // 16 * 16
    emb_rows = emb_in.shape[1]

    def e_parts(k):
        here = cols((r * T + plane(k)) * cw, cw)
        return (
            (emb_raw.at[0:straight, here], emb_in.at[k, 0:straight, :]),
            (emb_ref.at[:, here], emb_in.at[k, straight:emb_rows, :]),
        )

    def e_copy(k, p):
        src, dst = e_parts(k)[p]
        return remote(src, dst, e_send.at[k, p], e_recv.at[k, p], "tp", plane(k))

    e_own = [
        pltpu.make_async_copy(*e_parts(0)[p], e_send.at[0, p]) for p in range(2)
    ]
    e_own[0].start()
    for k in range(1, T):
        e_copy(k, 0).start()
    emb_blank = jnp.zeros((emb_rows - emb_raw.shape[0], nb // 2), F32)

    def tile_up(b, _):
        here = cols(b * (nb // 2), nb // 2)
        emb_ref[:, here] = jnp.concatenate(
            [emb_raw[straight : emb_raw.shape[0], here].astype(F32), emb_blank], axis=0
        ).astype(BF16)
        return 0

    lax.fori_loop(0, 2 * R, tile_up, 0)
    e_own[1].start()
    for k in range(1, T):
        e_copy(k, 1).start()

    row_at = lax.broadcasted_iota(jnp.int32, (rr, 128), 0)
    picked = row_at * 0
    for n in range(rr):
        picked = jnp.where(row_at == n, pick_ref[n], picked)
    picked = picked[:, :1]
    chosen = jnp.zeros((rr, kb), F32)
    for i in range(draft_len):
        chosen = jnp.where(picked == i, resid_ref[i * rr : (i + 1) * rr, :].astype(F32), chosen)
    racc_ref[...] = chosen.astype(BF16)

    home = t // ratio
    ra_offset = lax.rem(home - r + R, R)

    def ra_copy():
        return remote(racc_ref, racc_in.at[r], ra_send, ra_recv.at[ra_offset], "rep", home)

    @pl.when(home != r)
    def _():
        ra_copy().start()

    @pl.when(home == r)
    def _():
        racc_in[r] = racc_ref[...]

    w_copy = pltpu.make_async_copy(dproj_ref, w_buf, w_sem)
    w_copy.start()

    ws_copy(0, 0).start()
    ws_copy(0, 1).start()

    place_at = lax.broadcasted_iota(jnp.int32, (8 * rr, tokens), 0)
    token_at = lax.broadcasted_iota(jnp.int32, (8 * rr, tokens), 1)
    spread = (token_at == lax.rem(place_at, 8) * rr + place_at // 8) & (
        lax.rem(place_at, 8) < draft_len
    )
    padded[...] = jnp.dot(
        jnp.where(spread, 1.0, 0.0).astype(BF16), q_ref[...], preferred_element_type=F32
    )
    kv_copy.wait()
    tall = 8 * heads
    scale = HEAD_DIM ** (-0.5)
    token = lax.rem(lax.broadcasted_iota(jnp.int32, (tall, 128), 0), 8)
    fresh_ok = lax.broadcasted_iota(jnp.int32, (tall, 128), 1) <= token
    slots = kv_buf.shape[2]
    slot_at = lax.broadcasted_iota(jnp.int32, (tall, slots), 1)
    across = (((1,), (1,)), ((), ()))
    fresh_cols = cols(kv_group * HEAD_DIM, HEAD_DIM)
    unused = jnp.zeros((128 - draft_len, HEAD_DIM), F32)

    def attend_row(n, _):
        query = padded[pl.ds(pl.multiple_of(n * 8, 8), 8), :]
        query = jnp.concatenate(
            [query[:, h * HEAD_DIM : (h + 1) * HEAD_DIM] for h in range(heads)], axis=0
        ).astype(BF16)
        fresh_keys = jnp.concatenate(
            [fresh_ref[n, :, 0, fresh_cols].astype(F32), unused], axis=0
        ).astype(BF16)
        fresh_vals = jnp.concatenate(
            [fresh_ref[n, :, 1, fresh_cols].astype(F32), unused], axis=0
        ).astype(BF16)
        cache_scores = (
            lax.dot_general(query, kv_buf[n, 0], across, preferred_element_type=F32) * scale
        )
        fresh_scores = (
            lax.dot_general(query, fresh_keys, across, preferred_element_type=F32) * scale
        )
        cache_scores = jnp.where(slot_at < len_ref[n], cache_scores, -jnp.inf)
        fresh_scores = jnp.where(fresh_ok, fresh_scores, -jnp.inf)
        highest = jnp.maximum(
            jnp.max(cache_scores, axis=1, keepdims=True),
            jnp.max(fresh_scores, axis=1, keepdims=True),
        )
        cache_exp = jnp.exp(cache_scores - highest)
        fresh_exp = jnp.exp(fresh_scores - highest)
        total = jnp.sum(cache_exp, axis=1, keepdims=True) + jnp.sum(
            fresh_exp, axis=1, keepdims=True
        )
        mixed = jnp.dot(
            (cache_exp / total).astype(BF16), kv_buf[n, 1], preferred_element_type=F32
        ) + jnp.dot((fresh_exp / total).astype(BF16), fresh_vals, preferred_element_type=F32)
        padded[pl.ds(pl.multiple_of(n * 8, 8), 8), :] = jnp.concatenate(
            [mixed[h * 8 : (h + 1) * 8] for h in range(heads)], axis=1
        )
        return 0

    lax.fori_loop(0, rr, attend_row, 0, unroll=4)

    attended = padded[...].astype(BF16)
    row_at = lax.broadcasted_iota(jnp.int32, (rr, 8 * rr), 0)
    chosen = lax.broadcasted_iota(jnp.int32, (rr, 8 * rr), 1) == row_at * 8 + picked
    acc_ref[...] = jnp.dot(
        jnp.where(chosen, 1.0, 0.0).astype(BF16), attended, preferred_element_type=F32
    ).astype(BF16)

    def a_copy(j):
        return remote(acc_ref, acc_in.at[r], a_send.at[j], a_recv.at[j], "rep", tower(j))

    for j in range(1, R):
        a_copy(j).start()
    acc_in[r] = acc_ref[...]

    token_at = lax.broadcasted_iota(jnp.int32, (tokens, 8 * rr), 0)
    place_at = lax.broadcasted_iota(jnp.int32, (tokens, 8 * rr), 1)
    kept = (token_at == lax.rem(place_at, 8) * rr + place_at // 8) & (
        lax.rem(place_at, 8) < draft_len
    )
    attn_ref[...] = jnp.dot(
        jnp.where(kept, 1.0, 0.0).astype(BF16), attended, preferred_element_type=F32
    ).astype(BF16)


    for j in range(1, R):
        a_copy(j).wait_recv()

    @pl.when(home == r)
    def _():
        for j in range(1, R):
            remote(
                racc_ref, racc_in.at[tower_back(j)], ra_send, ra_recv.at[j], "rep", tower(j)
            ).wait_recv()

    wo_copy.wait()

    def q_copy(i, other):
        return remote(
            q_out.at[other],
            q_in.at[i, other],
            q_send.at[i, other],
            q_recv.at[i, other],
            "tp",
            chip * 2 + 1 - core,
        )

    def rs_copy(i, other):
        return remote(
            rs_out.at[other],
            rs_in.at[i, other],
            rs_send.at[i, other],
            rs_recv.at[i, other],
            "tp",
            flip(chip, other, chips) * 2 + core,
        )

    def sums(i, multiply, middle):
        def for_partner(other):
            q_out[other] = multiply(flip(chip, other, chips) * 2 + 1 - core)
            q_copy(i, other).start()

        def both(n, _):
            other = chips - 1 - n

            @pl.when(other > 0)
            def _():
                for_partner(other - 1)

            total = multiply(flip(chip, other, chips) * 2 + core)
            q_copy(i, other).wait_recv()
            total = (total + q_in[i, other]).astype(BF16)

            @pl.when(other > 0)
            def _():
                rs_out[other] = total
                rs_copy(i, other).start()

            @pl.when(other == 0)
            def _():
                rs_in[i, 0] = total

            return 0

        for_partner(chips - 1)
        lax.fori_loop(0, chips // 2, both, 0)
        middle()
        lax.fori_loop(chips // 2, chips, both, 0)

    def finish(i):
        total = rs_in[i, 0].astype(F32)
        for other in range(chips - 1, 0, -1):
            rs_copy(i, other).wait_recv()
            total = total + rs_in[i, other].astype(F32)
        return total

    def drain_sums(i):
        for other in range(chips):
            q_copy(i, other).wait_send()
            if other > 0:
                rs_copy(i, other).wait_send()

    first = acc_in[...].reshape(rows, acc_ref.shape[1])

    def project(c):
        part[...] = jnp.dot(first, wo_buf[:, cols(c * cw, cw)], preferred_element_type=F32)

        @pl.when(r * ratio + c // R == t)
        def _():
            part[...] += (
                racc_in[:, :, cols(lax.rem(c, R) * cw, cw)].reshape(rows, cw).astype(F32)
            )

        return part[...]

    sums(0, project, lambda: None)

    for copy in e_own:
        copy.wait()
    for k in range(1, T):
        for p in range(2):
            e_copy(k, p).wait_recv()

    def place(k, _):
        source = lax.rem(t - k + T, T)
        block = emb_in[k].astype(F32)
        for s in range(STEPS):
            emb_f[s, pl.ds(pl.multiple_of(source * own_rows, own_rows), own_rows), :] = block[
                s * own_rows : (s + 1) * own_rows
            ]
        return 0

    lax.fori_loop(0, T, place, 0)
    state[...] = finish(0).astype(BF16).astype(F32)
    w_copy.wait()

    gain_own = gain_ref[:, cols((r * T + t) * cw, cw)].astype(F32)
    gain_back = 1.0 / gain_ref[:, cols(t * kb, kb)].astype(F32)

    vb = min(kb, 512)

    def p_copy(n):
        return remote(
            p_out.at[n], p_in.at[n], p_send.at[n], p_recv.at[n], "tp", chip * 2 + 1 - core
        )

    def v_copy(n):
        return remote(
            v_out.at[n], v_in.at[n], v_send.at[n], v_recv.at[n], "tp", served(n, True)
        )

    def v_other(n):
        ws_copy(n, 0).wait()

        def block(b, _):
            here = cols(b * vb, vb)
            p_out[n, :, here] = jnp.dot(
                attn_ref[...], ws_buf[0, :, here], preferred_element_type=F32
            ).astype(BF16)
            return 0

        lax.fori_loop(0, kb // vb, block, 0)
        p_copy(n).start()

        @pl.when(n < chips - 1)
        def _():
            ws_copy(n + 1, 0).start()

    def v_own(n):
        ws_copy(n, 1).wait()
        p_copy(n).wait_recv()

        def block(b, _):
            here = cols(b * vb, vb)
            product = jnp.dot(attn_ref[...], ws_buf[1, :, here], preferred_element_type=F32)
            v_out[n, :, here] = (product + p_in[n, :, here].astype(F32)).astype(BF16)
            return 0

        lax.fori_loop(0, kb // vb, block, 0)

        @pl.when(n < chips - 1)
        def _():
            ws_copy(n + 1, 1).start()

    per_step = -(-chips // (STEPS - 1))

    def each_round(s, top, act):
        for i in range(per_step):
            n = s * per_step + i

            @pl.when((n >= 0) & (n < top))
            def _():
                act(n)

    def x_place(s, m, h):
        return x_buf.at[s, :, cols(m * cw + h * hw, hw)]

    def x_copy(s, h, j):
        q = tower_back(j)
        target = q * ratio + t // R
        m = lax.rem(t, R)
        return target, remote(
            z_buf.at[s, h, q],
            x_place(s, m, h),
            x_send.at[s, h, j],
            x_recv.at[s, m * halves + h],
            "tp",
            target,
        )

    def z_copy(s, h, j):
        return remote(
            z_buf.at[s, h, r],
            z_buf.at[s, h, r],
            z_send.at[s, h, j],
            z_recv.at[s, h, j],
            "rep",
            tower(j),
        )

    def z_arrival(s, h, j):
        q = tower_back(j)
        return remote(
            z_buf.at[s, h, q],
            z_buf.at[s, h, q],
            z_send.at[s, h, j],
            z_recv.at[s, h, j],
            "rep",
            tower(j),
        )

    def sq_copy(s, k):
        return remote(
            sq_out, sq_in.at[s, k], sq_send.at[s, k], sq_recv.at[s, k], "tp", plane(k)
        )

    def drain(s):
        for k in range(1, T):
            sq_copy(s, k).wait_send()
        for h in range(halves):
            for j in range(1, R):
                z_copy(s, h, j).wait_send()
            for j in range(R):
                target, copy = x_copy(s, h, j)

                @pl.when(target != t)
                def _():
                    copy.wait_send()

    def step(s, _):
        mixed = state[...] + emb_f[s]
        mixed = (mixed * gain_own).astype(BF16)
        for h in range(halves):
            z_buf[s, h, r] = mixed[:, h * hw : (h + 1) * hw]
        for h in range(halves):
            for j in range(1, R):
                z_copy(s, h, j).start()

        def forward(h, j):
            target, copy = x_copy(s, h, j)

            @pl.when(target != t)
            def _():
                copy.start()

            @pl.when(target == t)
            def _():
                x_buf[s, :, cols(lax.rem(t, R) * cw + h * hw, hw)] = z_buf[
                    s, h, tower_back(j)
                ]

        for h in range(halves):
            forward(h, 0)
        each_round(s - 1, chips - 1, lambda n: v_copy(n).start())
        drain_sums(s)

        @pl.when(s > 0)
        def _():
            drain(s - 1)

        each_round(s, chips, v_other)
        for h in range(halves):
            for j in range(1, R):
                z_arrival(s, h, j).wait_recv()
                forward(h, j)
        each_round(s, chips, v_own)

        for m in range(R):
            source = lax.rem(t, ratio) * R + m

            @pl.when(source != t)
            def _():
                for h in range(halves):
                    remote(
                        z_buf.at[s, h, 0],
                        x_place(s, m, h),
                        x_send.at[s, h, 0],
                        x_recv.at[s, m * halves + h],
                        "tp",
                        source,
                    ).wait_recv()

        def squares_out():
            lanes = jnp.zeros((rows, 128), F32)
            for b in range(kb // 128):
                here = slice(b * 128, (b + 1) * 128)
                plain = x_buf[s, :, here].astype(F32) * gain_back[:, here]
                lanes = lanes + plain * plain
            sq_out[:, :rows] = lax.dot_general(
                jnp.ones((8, 128), F32),
                lanes,
                (((1,), (1,)), ((), ())),
                precision=EXACT,
                preferred_element_type=F32,
            )
            for k in range(1, T):
                sq_copy(s, k).start()
            sq_in[s, 0] = sq_out[...]

        sums(
            s + 1,
            lambda c: jnp.dot(
                x_buf[s], w_buf[:, cols(c * cw, cw)], preferred_element_type=F32
            ),
            squares_out,
        )
        for k in range(1, T):
            sq_copy(s, k).wait_recv()
        squares = sq_in[s, 0]
        for k in range(1, T):
            squares = squares + sq_in[s, k]
        column = lax.dot_general(
            squares,
            jnp.full((8, 128), 0.125, F32),
            (((0,), (0,)), ((), ())),
            precision=EXACT,
            preferred_element_type=F32,
        )[:rows, :1]
        inverse = lax.rsqrt(column / width + 1e-05)
        update = finish(s + 1) * inverse
        state[...] += update / (1.0 + jnp.exp(-update))
        return 0

    sq_out[...] = jnp.zeros_like(sq_out)
    lax.fori_loop(0, STEPS, step, 0)
    drain_sums(STEPS)
    drain(STEPS - 1)

    def f_copy(k):
        return remote(f_out.at[k], f_in.at[t], f_send.at[k], f_recv.at[k], "tp", plane(k))

    blank = jnp.zeros((16 - own_rows, cw), F32)
    for k in range(T):
        here = pl.ds(pl.multiple_of(plane(k) * own_rows, own_rows), own_rows)
        f_out[k] = jnp.concatenate([state[here, :], blank], axis=0).astype(BF16)
        if k > 0:
            f_copy(k).start()
    f_in[t] = f_out[0]

    for k in range(1, T):
        remote(
            f_out.at[k],
            f_in.at[lax.rem(t - k + T, T)],
            f_send.at[k],
            f_recv.at[k],
            "tp",
            plane(k),
        ).wait()
    half = T // 2
    for k in range(half):
        top = f_in[k].astype(F32)[:own_rows]
        low = f_in[k + half].astype(F32)[:own_rows]
        g_buf[r, :, k * cw : (k + 1) * cw] = jnp.concatenate([top, low], axis=0).astype(BF16)

    def g_copy(j):
        return remote(g_buf.at[r], g_buf.at[r], g_send.at[j], g_recv.at[j], "rep", tower(j))

    for j in range(1, R):
        g_copy(j).start()

    def v_wait(n, _):
        v_copy(n).wait()
        return 0

    lax.fori_loop(0, chips - 1, v_wait, 0)

    def p_wait(n, _):
        p_copy(n).wait_send()
        return 0

    lax.fori_loop(0, chips, p_wait, 0)

    def v_sum(b, _):
        here = cols(b * vb, vb)
        total = v_out[chips - 1, :, here].astype(F32)
        for n in range(chips - 1):
            total = total + v_in[n, :, here].astype(F32)
        ver_ref[:, here] = (resid_ref[:, here].astype(F32) + total).astype(BF16)
        return 0

    lax.fori_loop(0, kb // vb, v_sum, 0)

    for j in range(1, R):
        q = tower_back(j)
        remote(g_buf.at[q], g_buf.at[q], g_send.at[j], g_recv.at[j], "rep", tower(j)).wait()
    for q in range(R):
        block = g_buf[q].astype(F32)
        out_ref[:, q * nb : q * nb + nb // 2] = block[:own_rows].astype(BF16)
        out_ref[:, q * nb + nb // 2 : (q + 1) * nb] = block[own_rows:].astype(BF16)

    for j in range(1, R):
        a_copy(j).wait_send()

    @pl.when(home != r)
    def _():
        ra_copy().wait_send()

    for k in range(1, T):
        for p in range(2):
            e_copy(k, p).wait_send()


def local(
    T,
    R,
    queries,
    kv_cache,
    kv_new,
    cache_len,
    out_proj,
    residual,
    accepted,
    draft_emb,
    draft_gain,
    draft_proj,
):
    row_count, draft_len, kdim = queries.shape
    width = draft_gain.shape[0]
    rows = row_count * R
    own_rows, steps = draft_emb.shape[:2]
    cw = width // (T * R)
    kb = width // T
    nb = width // R
    halves = 2 if cw >= 256 else 1
    emb_rows = -(-steps * own_rows // 16) * 16
    token_rows = row_count * draft_len
    dma = pltpu.SemaphoreType.DMA
    vmem = pl.BlockSpec(memory_space=pltpu.VMEM)
    smem = pl.BlockSpec(memory_space=pltpu.SMEM)
    hbm = pl.BlockSpec(memory_space=pl.ANY)
    verified, features = pl.pallas_call(
        functools.partial(fused, T, R, steps),
        out_shape=(
            jax.ShapeDtypeStruct((token_rows, kb), BF16),
            jax.ShapeDtypeStruct((own_rows, width), BF16),
        ),
        in_specs=[smem] * 2 + [vmem] * 5 + [hbm] * 3,
        out_specs=(vmem, vmem),
        scratch_shapes=[
            pltpu.VMEM((row_count, 2, kv_cache.shape[2], HEAD_DIM), BF16),
            pltpu.VMEM((8 * row_count, kdim), F32),
            pltpu.VMEM((token_rows, kdim), BF16),
            pltpu.VMEM((row_count, kdim), BF16),
            pltpu.VMEM((row_count, kb), BF16),
            pltpu.VMEM((16, width), BF16),
            pltpu.VMEM((kb, nb), BF16),
            pltpu.VMEM((kdim, nb), BF16),
            pltpu.VMEM((2, kdim, kb), BF16),
            pltpu.VMEM((T, emb_rows, cw), BF16),
            pltpu.VMEM((steps, rows, cw), F32),
            pltpu.VMEM((R, row_count, kdim), BF16),
            pltpu.VMEM((R, row_count, kb), BF16),
            pltpu.VMEM((rows, cw), F32),
            pltpu.VMEM((rows, cw), F32),
            pltpu.VMEM((T // 2, rows, cw), F32),
            pltpu.VMEM((steps + 1, T // 2, rows, cw), F32),
            pltpu.VMEM((T // 2, rows, cw), BF16),
            pltpu.VMEM((steps + 1, T // 2, rows, cw), BF16),
            pltpu.VMEM((8, 128), F32),
            pltpu.VMEM((steps, T, 8, 128), F32),
            pltpu.VMEM((steps, halves, R, rows, cw // halves), BF16),
            pltpu.VMEM((steps, rows, kb), BF16),
            pltpu.VMEM((T, 16, cw), BF16),
            pltpu.VMEM((T, 16, cw), BF16),
            pltpu.VMEM((R, 16, nb // 2), BF16),
            pltpu.VMEM((T // 2, token_rows, kb), BF16),
            pltpu.VMEM((T // 2, token_rows, kb), BF16),
            pltpu.VMEM((T // 2, token_rows, kb), BF16),
            pltpu.VMEM((T // 2, token_rows, kb), BF16),
            dma,
            dma,
            dma,
            dma((2,)),
            dma((T, 2)),
            dma((T, 2)),
            dma((R,)),
            dma((R,)),
            dma,
            dma((R,)),
            dma((steps + 1, T // 2)),
            dma((steps + 1, T // 2)),
            dma((steps + 1, T // 2)),
            dma((steps + 1, T // 2)),
            dma((steps, T)),
            dma((steps, T)),
            dma((steps, halves, R)),
            dma((steps, halves, R)),
            dma((steps, halves, R)),
            dma((steps, R * halves)),
            dma((T,)),
            dma((T,)),
            dma((R,)),
            dma((R,)),
            dma((T // 2,)),
            dma((T // 2,)),
            dma((T // 2,)),
            dma((T // 2,)),
        ],
        compiler_params=pltpu.CompilerParams(
            collective_id=0, has_side_effects=True, vmem_limit_bytes=56 * 2**20
        ),
        name="verify_and_draft",
    )(
        cache_len,
        accepted,
        queries.transpose(1, 0, 2).reshape(token_rows, kdim),
        kv_new.transpose(0, 2, 1, 3),
        residual.transpose(1, 0, 2).reshape(token_rows, kb),
        draft_gain.reshape(1, width),
        draft_emb.transpose(1, 0, 2).reshape(steps * own_rows, width),
        kv_cache,
        out_proj,
        draft_proj,
    )
    return verified.reshape(draft_len, row_count, kb).transpose(1, 0, 2), features


def solution(mesh):
    in_specs = (
        P("rep", None, "tp"),
        P("rep", None, None, None),
        P("rep", None, None, None),
        P("rep"),
        P("tp", None),
        P("rep", None, "tp"),
        P("rep"),
        P("tp", None, None),
        P(),
        P("tp", "rep"),
    )
    out_specs = (P("rep", None, "tp"), P("tp", None))
    body = functools.partial(local, mesh.shape["tp"], mesh.shape["rep"])
    return jax.shard_map(body, mesh=mesh, in_specs=in_specs, out_specs=out_specs, check_vma=False)
```

```python
import functools

import jax
import jax.numpy as jnp
from jax import lax
from jax.experimental import pallas as pl
from jax.experimental.pallas import tpu as pltpu
from jax.sharding import PartitionSpec as P

KV_HEADS = 4
HEAD_DIM = 128
MESH = pl.DeviceIdType.MESH
F32 = jnp.float32
BF16 = jnp.bfloat16
EXACT = lax.Precision.HIGHEST


def fused(
    T,
    R,
    STEPS,
    len_ref,
    pick_ref,
    q_ref,
    fresh_ref,
    resid_ref,
    gain_ref,
    emb_raw,
    kv_ref,
    oproj_ref,
    dproj_ref,
    ver_ref,
    out_ref,
    kv_buf,
    padded,
    mixed_ref,
    attn_ref,
    acc_ref,
    racc_ref,
    emb_ref,
    w_buf,
    wo_buf,
    ws_buf,
    emb_in,
    emb_f,
    acc_in,
    racc_in,
    part,
    state,
    q_out,
    q_in,
    rs_out,
    rs_in,
    sq_out,
    sq_in,
    z_buf,
    x_buf,
    f_out,
    f_in,
    g_buf,
    p_out,
    p_in,
    v_out,
    v_in,
    kv_sem,
    w_sem,
    wo_sem,
    ws_sem,
    e_send,
    e_recv,
    a_send,
    a_recv,
    ra_send,
    ra_recv,
    q_send,
    q_recv,
    rs_send,
    rs_recv,
    sq_send,
    sq_recv,
    z_send,
    z_recv,
    x_send,
    x_recv,
    f_send,
    f_recv,
    g_send,
    g_recv,
    p_send,
    p_recv,
    v_send,
    v_recv,
):
    t = lax.axis_index("tp")
    r = lax.axis_index("rep")
    ratio = T // R
    rows, cw = state.shape
    width = gain_ref.shape[1]
    kb = width // T
    nb = width // R
    own_rows = rows // T
    rr = acc_ref.shape[0]
    tokens, kdim = q_ref.shape
    draft_len = tokens // rr
    heads = kdim // HEAD_DIM
    chips = T // 2
    core = lax.rem(t, 2)
    chip = t // 2
    halves, hw = z_buf.shape[1], z_buf.shape[4]

    def plane(k):
        return lax.rem(t + k, T)

    def flip(index, k, limit):
        out, bit = 0, 1
        while bit < limit:
            out = out + bit * lax.rem(index // bit + k // bit, 2)
            bit *= 2
        return out

    def tower(j):
        return lax.rem(r + j, R)

    def tower_back(j):
        return lax.rem(r - j + R, R)

    def remote(src, dst, send, recv, axis, index):
        return pltpu.make_async_remote_copy(
            src_ref=src,
            dst_ref=dst,
            send_sem=send,
            recv_sem=recv,
            device_id={axis: index},
            device_id_type=MESH,
        )

    def cols(start, size):
        return pl.ds(pl.multiple_of(start, 128), size)

    kv_group = t * heads // (heads * T // KV_HEADS)
    kv_copy = pltpu.make_async_copy(
        kv_ref.at[:, :, :, cols(kv_group * HEAD_DIM, HEAD_DIM)], kv_buf, kv_sem
    )
    kv_copy.start()
    wo_copy = pltpu.make_async_copy(oproj_ref.at[:, cols(r * nb, nb)], wo_buf, wo_sem)
    wo_copy.start()

    def turn(n, own):
        k = chips - 1 - n
        swapped = (k // 4) * 4 + lax.rem(k, 2) * 2 + lax.rem(k // 2, 2)
        return k + (core if own else 1 - core) * (swapped - k)

    def served(n, own):
        return flip(chip, turn(n, own), chips) * 2 + (core if own else 1 - core)

    def ws_copy(n, own):
        return pltpu.make_async_copy(
            oproj_ref.at[:, cols(served(n, own) * kb, kb)], ws_buf.at[own], ws_sem.at[own]
        )

    barrier = pltpu.get_barrier_semaphore()
    for k in range(1, T):
        pl.semaphore_signal(barrier, inc=1, device_id={"tp": plane(k)}, device_id_type=MESH)
    for j in range(1, R):
        pl.semaphore_signal(barrier, inc=1, device_id={"rep": tower(j)}, device_id_type=MESH)
    pl.semaphore_wait(barrier, T - 1 + R - 1)

    straight = emb_raw.shape[0] // 16 * 16
    emb_rows = emb_in.shape[1]

    def e_parts(k):
        here = cols((r * T + plane(k)) * cw, cw)
        return (
            (emb_raw.at[0:straight, here], emb_in.at[k, 0:straight, :]),
            (emb_ref.at[:, here], emb_in.at[k, straight:emb_rows, :]),
        )

    def e_copy(k, p):
        src, dst = e_parts(k)[p]
        return remote(src, dst, e_send.at[k, p], e_recv.at[k, p], "tp", plane(k))

    e_own = [
        pltpu.make_async_copy(*e_parts(0)[p], e_send.at[0, p]) for p in range(2)
    ]
    e_own[0].start()
    for k in range(1, T):
        e_copy(k, 0).start()
    emb_blank = jnp.zeros((emb_rows - emb_raw.shape[0], nb // 2), F32)

    def tile_up(b, _):
        here = cols(b * (nb // 2), nb // 2)
        emb_ref[:, here] = jnp.concatenate(
            [emb_raw[straight : emb_raw.shape[0], here].astype(F32), emb_blank], axis=0
        ).astype(BF16)
        return 0

    lax.fori_loop(0, 2 * R, tile_up, 0)
    e_own[1].start()
    for k in range(1, T):
        e_copy(k, 1).start()

    row_at = lax.broadcasted_iota(jnp.int32, (rr, 128), 0)
    picked = row_at * 0
    for n in range(rr):
        picked = jnp.where(row_at == n, pick_ref[n], picked)
    picked = picked[:, :1]
    chosen = jnp.zeros((rr, kb), F32)
    for i in range(draft_len):
        chosen = jnp.where(picked == i, resid_ref[i * rr : (i + 1) * rr, :].astype(F32), chosen)
    racc_ref[...] = chosen.astype(BF16)

    home = t // ratio
    ra_offset = lax.rem(home - r + R, R)

    def ra_copy():
        return remote(racc_ref, racc_in.at[r], ra_send, ra_recv.at[ra_offset], "rep", home)

    @pl.when(home != r)
    def _():
        ra_copy().start()

    @pl.when(home == r)
    def _():
        racc_in[r] = racc_ref[...]

    w_copy = pltpu.make_async_copy(dproj_ref, w_buf, w_sem)
    w_copy.start()

    ws_copy(0, 0).start()
    ws_copy(0, 1).start()

    place_at = lax.broadcasted_iota(jnp.int32, (8 * rr, tokens), 0)
    token_at = lax.broadcasted_iota(jnp.int32, (8 * rr, tokens), 1)
    spread = (token_at == lax.rem(place_at, 8) * rr + place_at // 8) & (
        lax.rem(place_at, 8) < draft_len
    )
    padded[...] = jnp.dot(
        jnp.where(spread, 1.0, 0.0).astype(BF16), q_ref[...], preferred_element_type=F32
    )
    kv_copy.wait()
    tall = 8 * heads
    scale = HEAD_DIM ** (-0.5)
    token = lax.rem(lax.broadcasted_iota(jnp.int32, (tall, 128), 0), 8)
    fresh_ok = lax.broadcasted_iota(jnp.int32, (tall, 128), 1) <= token
    slots = kv_buf.shape[2]
    slot_at = lax.broadcasted_iota(jnp.int32, (tall, slots), 1)
    across = (((1,), (1,)), ((), ()))
    fresh_cols = cols(kv_group * HEAD_DIM, HEAD_DIM)
    unused = jnp.zeros((128 - draft_len, HEAD_DIM), F32)

    def stack(n):
        query = padded[pl.ds(pl.multiple_of(n * 8, 8), 8), :]
        return jnp.concatenate(
            [query[:, h * HEAD_DIM : (h + 1) * HEAD_DIM] for h in range(heads)], axis=0
        ).astype(BF16)

    def fresh(n, which):
        return jnp.concatenate(
            [fresh_ref[n, :, which, fresh_cols].astype(F32), unused], axis=0
        ).astype(BF16)

    def scores(query, keys):
        return lax.dot_general(query, keys, across, preferred_element_type=F32) * scale

    def attend_rows(group, _):
        members = [group * 4 + i for i in range(4)]
        queries = [stack(n) for n in members]
        cache_scores = [scores(q, kv_buf[n, 0]) for q, n in zip(queries, members)]
        fresh_scores = [scores(q, fresh(n, 0)) for q, n in zip(queries, members)]
        cache_scores = [
            jnp.where(slot_at < len_ref[n], x, -jnp.inf) for x, n in zip(cache_scores, members)
        ]
        fresh_scores = [jnp.where(fresh_ok, x, -jnp.inf) for x in fresh_scores]
        highest = [
            jnp.maximum(jnp.max(a, axis=1, keepdims=True), jnp.max(b, axis=1, keepdims=True))
            for a, b in zip(cache_scores, fresh_scores)
        ]
        cache_exp = [jnp.exp(a - m) for a, m in zip(cache_scores, highest)]
        fresh_exp = [jnp.exp(b - m) for b, m in zip(fresh_scores, highest)]
        total = [
            jnp.sum(a, axis=1, keepdims=True) + jnp.sum(b, axis=1, keepdims=True)
            for a, b in zip(cache_exp, fresh_exp)
        ]
        cache_weights = [(a / m).astype(BF16) for a, m in zip(cache_exp, total)]
        fresh_weights = [(b / m).astype(BF16) for b, m in zip(fresh_exp, total)]
        mixed = [
            jnp.dot(a, kv_buf[n, 1], preferred_element_type=F32)
            + jnp.dot(b, fresh(n, 1), preferred_element_type=F32)
            for a, b, n in zip(cache_weights, fresh_weights, members)
        ]
        mixed_ref[pl.ds(pl.multiple_of(group * 32, 32), 32), :] = jnp.concatenate(
            [
                jnp.concatenate([m[h * 8 : (h + 1) * 8] for h in range(heads)], axis=1)
                for m in mixed
            ],
            axis=0,
        )
        return 0

    lax.fori_loop(0, rr // 4, attend_rows, 0)

    attended = mixed_ref[...].astype(BF16)
    row_at = lax.broadcasted_iota(jnp.int32, (rr, 8 * rr), 0)
    chosen = lax.broadcasted_iota(jnp.int32, (rr, 8 * rr), 1) == row_at * 8 + picked
    acc_ref[...] = jnp.dot(
        jnp.where(chosen, 1.0, 0.0).astype(BF16), attended, preferred_element_type=F32
    ).astype(BF16)

    def a_copy(j):
        return remote(acc_ref, acc_in.at[r], a_send.at[j], a_recv.at[j], "rep", tower(j))

    for j in range(1, R):
        a_copy(j).start()
    acc_in[r] = acc_ref[...]

    token_at = lax.broadcasted_iota(jnp.int32, (tokens, 8 * rr), 0)
    place_at = lax.broadcasted_iota(jnp.int32, (tokens, 8 * rr), 1)
    kept = (token_at == lax.rem(place_at, 8) * rr + place_at // 8) & (
        lax.rem(place_at, 8) < draft_len
    )
    attn_ref[...] = jnp.dot(
        jnp.where(kept, 1.0, 0.0).astype(BF16), attended, preferred_element_type=F32
    ).astype(BF16)


    for j in range(1, R):
        a_copy(j).wait_recv()

    @pl.when(home == r)
    def _():
        for j in range(1, R):
            remote(
                racc_ref, racc_in.at[tower_back(j)], ra_send, ra_recv.at[j], "rep", tower(j)
            ).wait_recv()

    wo_copy.wait()

    def q_copy(i, other):
        return remote(
            q_out.at[other],
            q_in.at[i, other],
            q_send.at[i, other],
            q_recv.at[i, other],
            "tp",
            chip * 2 + 1 - core,
        )

    def rs_copy(i, other):
        return remote(
            rs_out.at[other],
            rs_in.at[i, other],
            rs_send.at[i, other],
            rs_recv.at[i, other],
            "tp",
            flip(chip, other, chips) * 2 + core,
        )

    def sums(i, multiply, middle):
        def for_partner(other):
            q_out[other] = multiply(flip(chip, other, chips) * 2 + 1 - core)
            q_copy(i, other).start()

        def both(n, _):
            other = chips - 1 - n

            @pl.when(other > 0)
            def _():
                for_partner(other - 1)

            total = multiply(flip(chip, other, chips) * 2 + core)
            q_copy(i, other).wait_recv()
            total = (total + q_in[i, other]).astype(BF16)

            @pl.when(other > 0)
            def _():
                rs_out[other] = total
                rs_copy(i, other).start()

            @pl.when(other == 0)
            def _():
                rs_in[i, 0] = total

            return 0

        for_partner(chips - 1)
        lax.fori_loop(0, chips // 2, both, 0)
        middle()
        lax.fori_loop(chips // 2, chips, both, 0)

    def finish(i):
        total = rs_in[i, 0].astype(F32)
        for other in range(chips - 1, 0, -1):
            rs_copy(i, other).wait_recv()
            total = total + rs_in[i, other].astype(F32)
        return total

    def drain_sums(i):
        for other in range(chips):
            q_copy(i, other).wait_send()
            if other > 0:
                rs_copy(i, other).wait_send()

    first = acc_in[...].reshape(rows, acc_ref.shape[1])

    def project(c):
        part[...] = jnp.dot(first, wo_buf[:, cols(c * cw, cw)], preferred_element_type=F32)

        @pl.when(r * ratio + c // R == t)
        def _():
            part[...] += (
                racc_in[:, :, cols(lax.rem(c, R) * cw, cw)].reshape(rows, cw).astype(F32)
            )

        return part[...]

    sums(0, project, lambda: None)

    for copy in e_own:
        copy.wait()
    for k in range(1, T):
        for p in range(2):
            e_copy(k, p).wait_recv()

    def place(k, _):
        source = lax.rem(t - k + T, T)
        block = emb_in[k].astype(F32)
        for s in range(STEPS):
            emb_f[s, pl.ds(pl.multiple_of(source * own_rows, own_rows), own_rows), :] = block[
                s * own_rows : (s + 1) * own_rows
            ]
        return 0

    lax.fori_loop(0, T, place, 0)
    state[...] = finish(0).astype(BF16).astype(F32)
    w_copy.wait()

    gain_own = gain_ref[:, cols((r * T + t) * cw, cw)].astype(F32)
    gain_back = 1.0 / gain_ref[:, cols(t * kb, kb)].astype(F32)

    vb = min(kb, 512)

    def p_copy(n):
        return remote(
            p_out.at[n], p_in.at[n], p_send.at[n], p_recv.at[n], "tp", chip * 2 + 1 - core
        )

    def v_copy(n):
        return remote(
            v_out.at[n], v_in.at[n], v_send.at[n], v_recv.at[n], "tp", served(n, True)
        )

    def v_other(n):
        ws_copy(n, 0).wait()

        def block(b, _):
            here = cols(b * vb, vb)
            p_out[n, :, here] = jnp.dot(
                attn_ref[...], ws_buf[0, :, here], preferred_element_type=F32
            ).astype(BF16)
            return 0

        lax.fori_loop(0, kb // vb, block, 0)
        p_copy(n).start()

        @pl.when(n < chips - 1)
        def _():
            ws_copy(n + 1, 0).start()

    def v_own(n):
        ws_copy(n, 1).wait()
        p_copy(n).wait_recv()

        def block(b, _):
            here = cols(b * vb, vb)
            product = jnp.dot(attn_ref[...], ws_buf[1, :, here], preferred_element_type=F32)
            v_out[n, :, here] = (product + p_in[n, :, here].astype(F32)).astype(BF16)
            return 0

        lax.fori_loop(0, kb // vb, block, 0)

        @pl.when(n < chips - 1)
        def _():
            ws_copy(n + 1, 1).start()

    per_step = -(-chips // (STEPS - 1))

    def each_round(s, top, act):
        for i in range(per_step):
            n = s * per_step + i

            @pl.when((n >= 0) & (n < top))
            def _():
                act(n)

    def x_place(s, m, h):
        return x_buf.at[s, :, cols(m * cw + h * hw, hw)]

    def x_copy(s, h, j):
        q = tower_back(j)
        target = q * ratio + t // R
        m = lax.rem(t, R)
        return target, remote(
            z_buf.at[s, h, q],
            x_place(s, m, h),
            x_send.at[s, h, j],
            x_recv.at[s, m * halves + h],
            "tp",
            target,
        )

    def z_copy(s, h, j):
        return remote(
            z_buf.at[s, h, r],
            z_buf.at[s, h, r],
            z_send.at[s, h, j],
            z_recv.at[s, h, j],
            "rep",
            tower(j),
        )

    def z_arrival(s, h, j):
        q = tower_back(j)
        return remote(
            z_buf.at[s, h, q],
            z_buf.at[s, h, q],
            z_send.at[s, h, j],
            z_recv.at[s, h, j],
            "rep",
            tower(j),
        )

    def sq_copy(s, k):
        return remote(
            sq_out, sq_in.at[s, k], sq_send.at[s, k], sq_recv.at[s, k], "tp", plane(k)
        )

    def drain(s):
        for k in range(1, T):
            sq_copy(s, k).wait_send()
        for h in range(halves):
            for j in range(1, R):
                z_copy(s, h, j).wait_send()
            for j in range(R):
                target, copy = x_copy(s, h, j)

                @pl.when(target != t)
                def _():
                    copy.wait_send()

    def step(s, _):
        mixed = state[...] + emb_f[s]
        mixed = (mixed * gain_own).astype(BF16)
        for h in range(halves):
            z_buf[s, h, r] = mixed[:, h * hw : (h + 1) * hw]
        for h in range(halves):
            for j in range(1, R):
                z_copy(s, h, j).start()

        def forward(h, j):
            target, copy = x_copy(s, h, j)

            @pl.when(target != t)
            def _():
                copy.start()

            @pl.when(target == t)
            def _():
                x_buf[s, :, cols(lax.rem(t, R) * cw + h * hw, hw)] = z_buf[
                    s, h, tower_back(j)
                ]

        for h in range(halves):
            forward(h, 0)
        each_round(s - 1, chips - 1, lambda n: v_copy(n).start())
        drain_sums(s)

        @pl.when(s > 0)
        def _():
            drain(s - 1)

        each_round(s, chips, v_other)
        for h in range(halves):
            for j in range(1, R):
                z_arrival(s, h, j).wait_recv()
                forward(h, j)
        each_round(s, chips, v_own)

        for m in range(R):
            source = lax.rem(t, ratio) * R + m

            @pl.when(source != t)
            def _():
                for h in range(halves):
                    remote(
                        z_buf.at[s, h, 0],
                        x_place(s, m, h),
                        x_send.at[s, h, 0],
                        x_recv.at[s, m * halves + h],
                        "tp",
                        source,
                    ).wait_recv()

        def squares_out():
            lanes = jnp.zeros((rows, 128), F32)
            for b in range(kb // 128):
                here = slice(b * 128, (b + 1) * 128)
                plain = x_buf[s, :, here].astype(F32) * gain_back[:, here]
                lanes = lanes + plain * plain
            sq_out[:, :rows] = lax.dot_general(
                jnp.ones((8, 128), F32),
                lanes,
                (((1,), (1,)), ((), ())),
                precision=EXACT,
                preferred_element_type=F32,
            )
            for k in range(1, T):
                sq_copy(s, k).start()
            sq_in[s, 0] = sq_out[...]

        sums(
            s + 1,
            lambda c: jnp.dot(
                x_buf[s], w_buf[:, cols(c * cw, cw)], preferred_element_type=F32
            ),
            squares_out,
        )
        for k in range(1, T):
            sq_copy(s, k).wait_recv()
        squares = sq_in[s, 0]
        for k in range(1, T):
            squares = squares + sq_in[s, k]
        column = lax.dot_general(
            squares,
            jnp.full((8, 128), 0.125, F32),
            (((0,), (0,)), ((), ())),
            precision=EXACT,
            preferred_element_type=F32,
        )[:rows, :1]
        inverse = lax.rsqrt(column / width + 1e-05)
        update = finish(s + 1) * inverse
        state[...] += update / (1.0 + jnp.exp(-update))
        return 0

    sq_out[...] = jnp.zeros_like(sq_out)
    lax.fori_loop(0, STEPS, step, 0)
    drain_sums(STEPS)
    drain(STEPS - 1)

    def f_copy(k):
        return remote(f_out.at[k], f_in.at[t], f_send.at[k], f_recv.at[k], "tp", plane(k))

    blank = jnp.zeros((16 - own_rows, cw), F32)
    for k in range(T):
        here = pl.ds(pl.multiple_of(plane(k) * own_rows, own_rows), own_rows)
        f_out[k] = jnp.concatenate([state[here, :], blank], axis=0).astype(BF16)
        if k > 0:
            f_copy(k).start()
    f_in[t] = f_out[0]

    for k in range(1, T):
        remote(
            f_out.at[k],
            f_in.at[lax.rem(t - k + T, T)],
            f_send.at[k],
            f_recv.at[k],
            "tp",
            plane(k),
        ).wait()
    half = T // 2
    for k in range(half):
        top = f_in[k].astype(F32)[:own_rows]
        low = f_in[k + half].astype(F32)[:own_rows]
        g_buf[r, :, k * cw : (k + 1) * cw] = jnp.concatenate([top, low], axis=0).astype(BF16)

    def g_copy(j):
        return remote(g_buf.at[r], g_buf.at[r], g_send.at[j], g_recv.at[j], "rep", tower(j))

    for j in range(1, R):
        g_copy(j).start()

    def v_wait(n, _):
        v_copy(n).wait()
        return 0

    lax.fori_loop(0, chips - 1, v_wait, 0)

    def p_wait(n, _):
        p_copy(n).wait_send()
        return 0

    lax.fori_loop(0, chips, p_wait, 0)

    def v_sum(b, _):
        here = cols(b * vb, vb)
        total = v_out[chips - 1, :, here].astype(F32)
        for n in range(chips - 1):
            total = total + v_in[n, :, here].astype(F32)
        ver_ref[:, here] = (resid_ref[:, here].astype(F32) + total).astype(BF16)
        return 0

    lax.fori_loop(0, kb // vb, v_sum, 0)

    for j in range(1, R):
        q = tower_back(j)
        remote(g_buf.at[q], g_buf.at[q], g_send.at[j], g_recv.at[j], "rep", tower(j)).wait()
    for q in range(R):
        block = g_buf[q].astype(F32)
        out_ref[:, q * nb : q * nb + nb // 2] = block[:own_rows].astype(BF16)
        out_ref[:, q * nb + nb // 2 : (q + 1) * nb] = block[own_rows:].astype(BF16)

    for j in range(1, R):
        a_copy(j).wait_send()

    @pl.when(home != r)
    def _():
        ra_copy().wait_send()

    for k in range(1, T):
        for p in range(2):
            e_copy(k, p).wait_send()


def local(
    T,
    R,
    queries,
    kv_cache,
    kv_new,
    cache_len,
    out_proj,
    residual,
    accepted,
    draft_emb,
    draft_gain,
    draft_proj,
):
    row_count, draft_len, kdim = queries.shape
    width = draft_gain.shape[0]
    rows = row_count * R
    own_rows, steps = draft_emb.shape[:2]
    cw = width // (T * R)
    kb = width // T
    nb = width // R
    halves = 2 if cw >= 256 else 1
    emb_rows = -(-steps * own_rows // 16) * 16
    token_rows = row_count * draft_len
    dma = pltpu.SemaphoreType.DMA
    vmem = pl.BlockSpec(memory_space=pltpu.VMEM)
    smem = pl.BlockSpec(memory_space=pltpu.SMEM)
    hbm = pl.BlockSpec(memory_space=pl.ANY)
    verified, features = pl.pallas_call(
        functools.partial(fused, T, R, steps),
        out_shape=(
            jax.ShapeDtypeStruct((token_rows, kb), BF16),
            jax.ShapeDtypeStruct((own_rows, width), BF16),
        ),
        in_specs=[smem] * 2 + [vmem] * 5 + [hbm] * 3,
        out_specs=(vmem, vmem),
        scratch_shapes=[
            pltpu.VMEM((row_count, 2, kv_cache.shape[2], HEAD_DIM), BF16),
            pltpu.VMEM((8 * row_count, kdim), F32),
            pltpu.VMEM((8 * row_count, kdim), F32),
            pltpu.VMEM((token_rows, kdim), BF16),
            pltpu.VMEM((row_count, kdim), BF16),
            pltpu.VMEM((row_count, kb), BF16),
            pltpu.VMEM((16, width), BF16),
            pltpu.VMEM((kb, nb), BF16),
            pltpu.VMEM((kdim, nb), BF16),
            pltpu.VMEM((2, kdim, kb), BF16),
            pltpu.VMEM((T, emb_rows, cw), BF16),
            pltpu.VMEM((steps, rows, cw), F32),
            pltpu.VMEM((R, row_count, kdim), BF16),
            pltpu.VMEM((R, row_count, kb), BF16),
            pltpu.VMEM((rows, cw), F32),
            pltpu.VMEM((rows, cw), F32),
            pltpu.VMEM((T // 2, rows, cw), F32),
            pltpu.VMEM((steps + 1, T // 2, rows, cw), F32),
            pltpu.VMEM((T // 2, rows, cw), BF16),
            pltpu.VMEM((steps + 1, T // 2, rows, cw), BF16),
            pltpu.VMEM((8, 128), F32),
            pltpu.VMEM((steps, T, 8, 128), F32),
            pltpu.VMEM((steps, halves, R, rows, cw // halves), BF16),
            pltpu.VMEM((steps, rows, kb), BF16),
            pltpu.VMEM((T, 16, cw), BF16),
            pltpu.VMEM((T, 16, cw), BF16),
            pltpu.VMEM((R, 16, nb // 2), BF16),
            pltpu.VMEM((T // 2, token_rows, kb), BF16),
            pltpu.VMEM((T // 2, token_rows, kb), BF16),
            pltpu.VMEM((T // 2, token_rows, kb), BF16),
            pltpu.VMEM((T // 2, token_rows, kb), BF16),
            dma,
            dma,
            dma,
            dma((2,)),
            dma((T, 2)),
            dma((T, 2)),
            dma((R,)),
            dma((R,)),
            dma,
            dma((R,)),
            dma((steps + 1, T // 2)),
            dma((steps + 1, T // 2)),
            dma((steps + 1, T // 2)),
            dma((steps + 1, T // 2)),
            dma((steps, T)),
            dma((steps, T)),
            dma((steps, halves, R)),
            dma((steps, halves, R)),
            dma((steps, halves, R)),
            dma((steps, R * halves)),
            dma((T,)),
            dma((T,)),
            dma((R,)),
            dma((R,)),
            dma((T // 2,)),
            dma((T // 2,)),
            dma((T // 2,)),
            dma((T // 2,)),
        ],
        compiler_params=pltpu.CompilerParams(
            collective_id=0, has_side_effects=True, vmem_limit_bytes=56 * 2**20
        ),
        name="verify_and_draft",
    )(
        cache_len,
        accepted,
        queries.transpose(1, 0, 2).reshape(token_rows, kdim),
        kv_new.transpose(0, 2, 1, 3),
        residual.transpose(1, 0, 2).reshape(token_rows, kb),
        draft_gain.reshape(1, width),
        draft_emb.transpose(1, 0, 2).reshape(steps * own_rows, width),
        kv_cache,
        out_proj,
        draft_proj,
    )
    return verified.reshape(draft_len, row_count, kb).transpose(1, 0, 2), features


def solution(mesh):
    in_specs = (
        P("rep", None, "tp"),
        P("rep", None, None, None),
        P("rep", None, None, None),
        P("rep"),
        P("tp", None),
        P("rep", None, "tp"),
        P("rep"),
        P("tp", None, None),
        P(),
        P("tp", "rep"),
    )
    out_specs = (P("rep", None, "tp"), P("tp", None))
    body = functools.partial(local, mesh.shape["tp"], mesh.shape["rep"])
    return jax.shard_map(body, mesh=mesh, in_specs=in_specs, out_specs=out_specs, check_vma=False)
```
